32 devices in a mesh: group: 2 (over y), tile: 8 (over z, x), lev: 2 (over core).
Axes of the slice: x: 2, y: 2, z: 4, core: 2. Of those that a mesh axis runs over, the one named last changes fastest.
Arguments:
- members_x: bfloat16 [80, 32, 32768], P(None, 'lev', ('group', 'tile')), parts along dimension 2, may hold values from -6 to 6
- error_early: bfloat16 [32, 32768], P('lev', ('group', 'tile')), parts along dimension 1, may hold values from -6 to 6
- error_late: bfloat16 [32, 32768], P('lev', ('group', 'tile')), parts along dimension 1, may hold values from -6 to 6
- energy: bfloat16 [32, 32768], P('lev', ('group', 'tile')), parts along dimension 1, may hold values from 0.29882812 to 3
- vert_weight: float32 [8, 32], replicated, may hold values from 0.05 to 1
- tile_lists: int32 [16, 2, 3], P(('group', 'tile')), parts along dimension 0, may hold values from 0 to 7, as said below
- obs_block: int32 [16, 4096], P(('group', 'tile')), parts along dimension 0, may hold values from 0 to 1, never falling along the last dimension, each value on 1 to 4095 neighbouring positions
- obs_bin: int32 [16, 4096], P(('group', 'tile')), parts along dimension 0, may hold values from 0 to 7
- obs_column: int32 [16, 4096], P(('group', 'tile')), parts along dimension 0, may hold values from 0 to 2047
- obs_pert: bfloat16 [16, 80, 4096], P(('group', 'tile')), parts along dimension 0, may hold values from -6 to 6
- innovation: float32 [16, 4096], P(('group', 'tile')), parts along dimension 0, may hold values from -6 to 6
- inv_variance: float32 [16, 4096], P(('group', 'tile')), parts along dimension 0, may hold values from 0.25 to 4
- horiz_weight: float32 [16, 4, 4096], P(('group', 'tile')), parts along dimension 0, may hold values from 0.1 to 1
Outputs:
- impact: float32 [16, 2048, 2], P(('group', 'tile'), None, 'lev'), parts along dimension 0
The draws below stay inside these ranges and needn't reach their ends.
There are 2 independent parts, one for each index of `group`. The reference program is written for one: setup_inputs(seed, part) draws one part's arguments, and reference() takes and returns one part's arrays. A program takes and returns all parts, laid end to end along the dimension named above; an argument that names none is the same for every part. Nothing has to cross between parts.
Inputs may be any that keep to these rules, and one draw needn't show every extreme that they name: `tile_lists`: in each row, the 2 * (3) entries are distinct tiles and none is the row's own tile. `obs_block`: within a row block numbers never fall; every block of a row holds 1 to 4095 observations.
All inputs are finite; a program needn't handle non-finite values.
Results may differ from the reference program's by a relative error of at most 0.0029.
Values may be sent and summed in bfloat16 or wider, within the bound.
A program may use at most 64 MiB of HBM per device.

```python
import math
import jax
import jax.numpy as jnp
import numpy as np
from jax import lax

K = 80
BINS = 8
NL = 4
C_DEV = 2048
OBS_DEV = 4096
LEVELS = 32
COLUMNS = 16384
BLK_DEV = 2
MOST = 4095
N_TILE = 8
N_LEV = 2


def draw_tile_lists(key, part):
    key = jax.random.fold_in(key, 7)
    row_keys = jax.random.split(key, N_TILE)

    def device_row(row_key, device_number):
        shuffled = jax.random.permutation(row_key, N_TILE - 1)[:BLK_DEV * (NL - 1)]
        return ((device_number + 1 + shuffled) % N_TILE).reshape(BLK_DEV, NL - 1).astype(jnp.int32)
    return jax.vmap(device_row)(row_keys, jnp.arange(N_TILE, dtype=jnp.int32))


def place_ends(array, rng, low, largest):
    dims = array.shape
    place = [jax.random.randint(jax.random.fold_in(rng, axis), (), 0, dims[axis]) for axis in range(len(dims))]
    array = array.at[tuple(place)].set(low)
    longest = dims.index(max(dims))
    place[longest] = (place[longest] + 1) % dims[longest]
    return array.at[tuple(place)].set(largest)


def level_of(own_key, extent, cuts, smallest, top_value):
    factor_of, own = 1.0, jax.random.fold_in(own_key, 6)
    for position, blocks in cuts:
        draws = jnp.exp(jax.random.uniform(jax.random.fold_in(own, position), (blocks,), jnp.float32, smallest / len(cuts), top_value / len(cuts)))
        factor_of = factor_of * jnp.repeat(draws, extent[position] // blocks).reshape([-1 if axis == position else 1 for axis in range(len(extent))])
    return factor_of


def length_profile(count, total, most, skew):
    loads = [(1 << 20) // math.isqrt(standing ** skew) + 1 for standing in range(2, count + 1)]
    surplus, given = total - most - (count - 1), [1] * (count - 1)
    while surplus > 0:
        candidates = [i for i in range(count - 1) if given[i] < most]
        pool, left = sum([loads[i] for i in candidates]), surplus
        for i in candidates:
            more = min(most - given[i], max(1, left * loads[i] // pool), surplus)
            given[i] = given[i] + more
            surplus = surplus - more
    return np.array([most] + given)


def uneven(key, number_of, total, bound, slope):
    if number_of == 2:
        one = jax.random.randint(key, (), max(1, total - bound), min(bound, total - 1) + 1)
        return jnp.stack([one, total - one])
    sizes = jnp.asarray(length_profile(number_of, total, bound, slope), jnp.int32)
    twos = (number_of - 1) // 2
    donor, sink = sizes[1:1 + 2 * twos:2], sizes[2:2 + 2 * twos:2]
    slack = jnp.minimum(donor - 1, bound - sink)
    shifted = jax.random.randint(jax.random.fold_in(key, 1), (twos,), 0, 1 << 20) % (slack + 1)
    sizes = sizes.at[1:1 + 2 * twos:2].set(donor - shifted).at[2:2 + 2 * twos:2].set(sink + shifted)
    return sizes[jax.random.permutation(jax.random.fold_in(key, 2), number_of)]


def gaussian(key, dims, spread, limit, shards=(), kind=jnp.bfloat16):
    array = jax.random.normal(key, dims, jnp.float32) * spread
    if len(shards) > 0:
        array = level_of(key, dims, shards, -0.22, 0.18) * array
    return jnp.clip(array, min=-limit, max=limit).astype(kind)


def setup_inputs(seed: int = 0, part: int = 0) -> dict:
    key_list = jax.random.split(jax.random.key(seed), 14)
    part_keys = jax.random.split(jax.random.fold_in(key_list[13], part), 14)
    members_x = gaussian(part_keys[0], (K, LEVELS, COLUMNS), 1.0, 6.0, ((1, 2), (2, 8)))
    error_early = gaussian(part_keys[1], (LEVELS, COLUMNS), 1.0, 6.0, ((0, 2), (1, 8)))
    error_late = gaussian(part_keys[2], (LEVELS, COLUMNS), 1.0, 6.0, ((0, 2), (1, 8)))
    energy = jnp.clip(jnp.exp(math.log(3.0) - 2.306499 * jax.random.uniform(part_keys[3], (LEVELS, COLUMNS), jnp.float32) ** level_of(part_keys[3], (LEVELS, COLUMNS), ((0, 2), (1, 8)), -0.2, 0.2)), 0.29882812, 3.0).astype(jnp.bfloat16)
    vert_weight = jnp.clip(jax.random.uniform(key_list[4], (BINS, LEVELS), jnp.float32, 0.05, 1.0), 0.05, 1.0)
    tile_lists = draw_tile_lists(jax.random.fold_in(jax.random.fold_in(key_list[13], part), 71), part)
    obs_block = jax.vmap(lambda own: jnp.searchsorted(jnp.cumsum(uneven(own, BLK_DEV, OBS_DEV, MOST, 2)), jnp.arange(OBS_DEV), side="right"))(jax.random.split(part_keys[6], N_TILE)).reshape((N_TILE, OBS_DEV)).astype(jnp.int32)
    obs_bin = place_ends(jax.random.randint(part_keys[7], (N_TILE, OBS_DEV), 0, BINS), jax.random.fold_in(part_keys[7], 1), 0, BINS - 1).astype(jnp.int32)
    obs_column = place_ends(jax.random.randint(part_keys[8], (N_TILE, OBS_DEV), 0, C_DEV), jax.random.fold_in(part_keys[8], 1), 0, C_DEV - 1).astype(jnp.int32)
    obs_pert = gaussian(part_keys[9], (N_TILE, K, OBS_DEV), 1.0, 6.0, ((0, 8),))
    innovation = gaussian(part_keys[10], (N_TILE, OBS_DEV), 1.0, 6.0, ((0, 8),), jnp.float32)
    inv_variance = jnp.clip(jnp.exp(math.log(4.0) - 2.7725887 * jax.random.uniform(part_keys[11], (N_TILE, OBS_DEV), jnp.float32) ** level_of(part_keys[11], (N_TILE, OBS_DEV), ((0, 8),), -0.2, 0.2)), 0.25, 4.0)
    horiz_weight = jnp.clip(0.1 + 0.9 * jax.random.uniform(part_keys[12], (N_TILE, NL, OBS_DEV), jnp.float32) ** level_of(part_keys[12], (N_TILE, NL, OBS_DEV), ((0, 8),), -0.2, 0.2), 0.1, 1.0)
    return dict(members_x=members_x, error_early=error_early, error_late=error_late, energy=energy, vert_weight=vert_weight, tile_lists=tile_lists, obs_block=obs_block, obs_bin=obs_bin, obs_column=obs_column, obs_pert=obs_pert, innovation=innovation, inv_variance=inv_variance, horiz_weight=horiz_weight)


def reference(members_x, error_early, error_late, energy, vert_weight, tile_lists, obs_block, obs_bin, obs_column, obs_pert, innovation, inv_variance, horiz_weight):
    scaled = energy.astype(jnp.float32) * (error_early.astype(jnp.float32) + error_late.astype(jnp.float32))

    def one_tile(tile_number):
        start = (tile_number * C_DEV).astype(jnp.int32)
        block_x = lax.dynamic_slice_in_dim(members_x, start, C_DEV, 2).astype(jnp.float32)
        block_scale = lax.dynamic_slice_in_dim(scaled, start, C_DEV, 1)
        weighted = block_x * block_scale[None]
        summed = jnp.einsum("bl,klc->kbc", vert_weight, weighted, precision=lax.Precision.HIGHEST)
        return summed.astype(jnp.bfloat16).reshape(K, BINS * C_DEV)

    summary = lax.map(one_tile, jnp.arange(N_TILE, dtype=jnp.int32))

    def one_owner(owner):
        blocks_here = obs_block[owner]
        lookup_place = obs_bin[owner] * C_DEV + obs_column[owner]
        pert_here = obs_pert[owner].astype(jnp.float32)
        total = jnp.zeros((OBS_DEV,), jnp.float32)
        for entry in range(NL):
            if entry == 0:
                tiles = jnp.full((OBS_DEV,), owner, jnp.int32)
            else:
                tiles = tile_lists[owner][blocks_here, entry - 1].astype(jnp.int32)
            values = summary[tiles, :, lookup_place].astype(jnp.float32)
            dots = jnp.sum(values * pert_here.T, axis=1)
            total = total + horiz_weight[owner, entry] * dots
        return innovation[owner] * inv_variance[owner] / (K - 1.0) * total

    result = lax.map(one_owner, jnp.arange(N_TILE, dtype=jnp.int32))
    return result.reshape(N_TILE, OBS_DEV // N_LEV, N_LEV)
```

```python
import functools

import jax
import jax.numpy as jnp
from jax import lax
from jax.experimental import pallas as pl
from jax.experimental.pallas import tpu as pltpu
from jax.sharding import PartitionSpec as P

CHUNK = 256
LANES = 128
VMEM_LIMIT = 56 * 1024 * 1024


def pick_level(values, lev_place, lev_count):
    shaped = values.reshape(values.shape[:-1] + (values.shape[-1] // lev_count, lev_count))
    return lax.dynamic_slice_in_dim(shaped, lev_place, 1, shaped.ndim - 1)[..., 0]


def split_high_low(values):
    high = values.astype(jnp.bfloat16)
    low = (values - high.astype(jnp.float32)).astype(jnp.bfloat16)
    return high, low


def partial_kernel(group, members_ref, early_ref, late_ref, energy_ref, weight_ref, own_ref, sent_ref):
    members, levels, width = members_ref.shape
    bins = own_ref.shape[0]
    scaled = energy_ref[...].astype(jnp.float32) * (
        early_ref[...].astype(jnp.float32) + late_ref[...].astype(jnp.float32)
    )
    rows = bins * group
    weight = weight_ref[...]
    for part in range(members // group):
        block = members_ref[part * group:(part + 1) * group].astype(jnp.float32) * scaled[None]
        high, low = split_high_low(block.reshape(group * levels, width))
        both = jnp.dot(weight, high, preferred_element_type=jnp.float32)
        summed = both[:rows] + both[rows:]
        summed = summed + jnp.dot(weight[:rows], low, preferred_element_type=jnp.float32)
        shaped = summed.reshape(bins, group, width)
        own_ref[:, part * group:(part + 1) * group, :] = shaped
        sent_ref[:, part * group:(part + 1) * group, :] = shaped.astype(jnp.bfloat16)


def partial_summary(members_x, error_early, error_late, energy, local_vert):
    members, levels, columns = members_x.shape
    bins = local_vert.shape[0]
    group = 16
    width = min(512, columns)
    eye = jnp.eye(group, dtype=jnp.float32)
    weight = (local_vert[:, None, None, :] * eye[None, :, :, None]).reshape(bins * group, group * levels)
    weight = jnp.concatenate(split_high_low(weight), axis=0)
    field = pl.BlockSpec((levels, width), lambda i: (0, i))
    out = pl.BlockSpec((bins, members, width), lambda i: (0, 0, i))
    return pl.pallas_call(
        functools.partial(partial_kernel, group),
        grid=(columns // width,),
        in_specs=[
            pl.BlockSpec((members, levels, width), lambda i: (0, 0, i)),
            field,
            field,
            field,
            pl.BlockSpec(weight.shape, lambda i: (0, 0)),
        ],
        out_specs=[out, out],
        out_shape=[
            jax.ShapeDtypeStruct((bins, members, columns), jnp.float32),
            jax.ShapeDtypeStruct((bins, members, columns), jnp.bfloat16),
        ],
        compiler_params=pltpu.CompilerParams(vmem_limit_bytes=VMEM_LIMIT),
        name="partial_summary",
    )(members_x, error_early, error_late, energy, weight)


def dots_kernel(bins, first_ref, last_ref, own_ref, other_ref, lookup_ref, pert_ref, dots_ref, table_ref, rows_ref):
    step = pl.program_id(0)
    members, columns = own_ref.shape[1], own_ref.shape[2]

    @pl.when(step < bins)
    def _():
        for start in range(0, columns, LANES):
            here = slice(start, start + LANES)
            summed = own_ref[0, :, here] + other_ref[0, :, here].astype(jnp.float32)
            padded = jnp.concatenate(
                [summed, jnp.zeros((LANES - members, LANES), jnp.float32)], axis=0
            )
            place = pl.multiple_of(step * columns + start, LANES)
            table_ref[pl.ds(place, LANES), :] = padded.T

    @pl.when(step >= bins)
    def _():
        owner = step - bins
        dots_ref[...] = jnp.zeros_like(dots_ref)
        row_id = lax.broadcasted_iota(jnp.int32, (LANES, LANES), 0)
        col_id = lax.broadcasted_iota(jnp.int32, (LANES, LANES), 1)

        def one_chunk(chunk, carry):
            base = pl.multiple_of(chunk * CHUNK, CHUNK)
            for place in range(CHUNK):
                index = lookup_ref[0, 0, base + place]
                rows_ref[pl.ds(place, 1), :] = table_ref[pl.ds(index, 1), :]
            for sub in range(0, CHUNK, LANES):
                values = rows_ref[sub:sub + LANES, :members]
                high, low = split_high_low(values)
                here = pl.ds(pl.multiple_of(base + sub, LANES), LANES)
                pert = pert_ref[0, :, here]
                product = jnp.dot(high, pert, preferred_element_type=jnp.float32) + jnp.dot(
                    low, pert, preferred_element_type=jnp.float32
                )
                picked = jnp.where(row_id == col_id, product, 0.0)
                dots_ref[0, :, here] = jnp.sum(picked, axis=0, keepdims=True)
            return carry

        lax.fori_loop(first_ref[owner], last_ref[owner], one_chunk, 0)


def tile_dots(own, other, lookups, perts, first, last):
    bins, members, columns = own.shape
    peers, _, share = lookups.shape
    return pl.pallas_call(
        functools.partial(dots_kernel, bins),
        grid_spec=pltpu.PrefetchScalarGridSpec(
            num_scalar_prefetch=2,
            grid=(bins + peers,),
            in_specs=[
                pl.BlockSpec((1, members, columns), lambda i, *_: (jnp.minimum(i, bins - 1), 0, 0)),
                pl.BlockSpec((1, members, columns), lambda i, *_: (jnp.minimum(i, bins - 1), 0, 0)),
                pl.BlockSpec(
                    (1, 1, share), lambda i, *_: (jnp.maximum(i - bins, 0), 0, 0), memory_space=pltpu.SMEM
                ),
                pl.BlockSpec((1, members, share), lambda i, *_: (jnp.maximum(i - bins, 0), 0, 0)),
            ],
            out_specs=pl.BlockSpec((1, 1, share), lambda i, *_: (jnp.maximum(i - bins, 0), 0, 0)),
            scratch_shapes=[
                pltpu.VMEM((bins * columns, LANES), jnp.float32),
                pltpu.VMEM((CHUNK, LANES), jnp.float32),
            ],
        ),
        out_shape=jax.ShapeDtypeStruct((peers, 1, share), jnp.float32),
        compiler_params=pltpu.CompilerParams(vmem_limit_bytes=VMEM_LIMIT),
        name="tile_dots",
    )(first, last, own, other, lookups, perts)


def on_device(
    members_x,
    error_early,
    error_late,
    energy,
    vert_weight,
    tile_lists,
    obs_block,
    obs_bin,
    obs_column,
    obs_pert,
    innovation,
    inv_variance,
    horiz_weight,
):
    lev_count = lax.axis_size("lev")
    lev_place = lax.axis_index("lev")
    peers = lax.axis_size("tile")
    tile_place = lax.axis_index("tile")
    members = members_x.shape[0]
    levels_here = members_x.shape[1]
    columns = members_x.shape[2]
    tile_table = tile_lists[0]
    blocks = tile_table.shape[0]
    later_slots = tile_table.shape[1]
    obs_count = obs_block.shape[1]
    share = obs_count // lev_count

    half = lev_place * share
    perts = lax.all_gather(lax.dynamic_slice_in_dim(obs_pert[0], half, share, 1), "tile")
    lookup_half = lax.dynamic_slice_in_dim(obs_bin[0] * columns + obs_column[0], half, share, 0)

    tile_ids = jnp.arange(peers, dtype=jnp.int32)
    block_ids = jnp.arange(blocks, dtype=jnp.int32)
    starts = jnp.sum((obs_block[0][None, :] < block_ids[:, None]).astype(jnp.int32), axis=1)
    ends = jnp.sum((obs_block[0][None, :] <= block_ids[:, None]).astype(jnp.int32), axis=1)
    listed = jnp.any(tile_table[:, :, None] == tile_ids[None, None, :], axis=1)
    range_first = jnp.sum(jnp.where(listed, starts[:, None], 0), axis=0)
    range_last = jnp.sum(jnp.where(listed, ends[:, None], 0), axis=0)
    range_first = jnp.where(tile_ids == tile_place, 0, range_first)
    range_last = jnp.where(tile_ids == tile_place, obs_count, range_last)
    range_first = jnp.clip(range_first - half, 0, share)
    range_last = jnp.clip(range_last - half, 0, share)
    packed = jnp.concatenate([lookup_half, range_first, range_last])
    everyone = lax.all_gather(packed, "tile")
    lookups = everyone[:, :share].reshape(peers, 1, share)
    first = lax.dynamic_slice_in_dim(everyone, share + tile_place, 1, 1)[:, 0]
    last = lax.dynamic_slice_in_dim(everyone, share + peers + tile_place, 1, 1)[:, 0]
    first_chunk = first // CHUNK
    last_chunk = jnp.where(last > first, (last + CHUNK - 1) // CHUNK, first_chunk)

    local_vert = lax.dynamic_slice_in_dim(vert_weight, lev_place * levels_here, levels_here, 1)
    own, sent = partial_summary(members_x, error_early, error_late, energy, local_vert)
    other = lax.ppermute(sent, "lev", [(i, (i + 1) % lev_count) for i in range(lev_count)])
    dots = tile_dots(own, other, lookups, perts, first_chunk, last_chunk)

    by_parity = jnp.moveaxis(dots.reshape(peers, share // lev_count, lev_count), 2, 1)
    by_parity = by_parity.reshape(peers * lev_count, share // lev_count)
    returned = lax.all_to_all(by_parity, ("tile", "lev"), split_axis=0, concat_axis=0, tiled=True)
    returned = returned.reshape(peers, share)

    block_mine = pick_level(obs_block[0], lev_place, lev_count)
    weight_mine = pick_level(horiz_weight[0], lev_place, lev_count)
    block_onehot = (block_mine[:, None] == block_ids[None, :]).astype(jnp.int32)
    total = jnp.where(tile_ids[:, None] == tile_place, weight_mine[0][None, :], 0.0)
    for entry in range(1, later_slots + 1):
        peer_mine = jnp.sum(block_onehot * tile_table[:, entry - 1][None, :], axis=1)
        total = total + jnp.where(
            tile_ids[:, None] == peer_mine[None, :], weight_mine[entry][None, :], 0.0
        )
    obs_scale = (
        pick_level(innovation[0], lev_place, lev_count)
        * pick_level(inv_variance[0], lev_place, lev_count)
        / (members - 1.0)
    )
    impact = obs_scale * jnp.sum(total * returned, axis=0)
    return impact[None, :, None]


def solution(mesh):
    return jax.shard_map(
        on_device,
        mesh=mesh,
        in_specs=(
            P(None, "lev", ("group", "tile")),
            P("lev", ("group", "tile")),
            P("lev", ("group", "tile")),
            P("lev", ("group", "tile")),
            P(),
            P(("group", "tile"), None, None),
            P(("group", "tile"), None),
            P(("group", "tile"), None),
            P(("group", "tile"), None),
            P(("group", "tile"), None, None),
            P(("group", "tile"), None),
            P(("group", "tile"), None),
            P(("group", "tile"), None, None),
        ),
        out_specs=P(("group", "tile"), None, "lev"),
        check_vma=False,
    )
```

```python
import functools

import jax
import jax.numpy as jnp
from jax import lax
from jax.experimental import pallas as pl
from jax.experimental.pallas import tpu as pltpu
from jax.sharding import PartitionSpec as P

CHUNK = 256
LANES = 128
VMEM_LIMIT = 56 * 1024 * 1024


def split_high_low(values):
    high = values.astype(jnp.bfloat16)
    low = (values - high.astype(jnp.float32)).astype(jnp.bfloat16)
    return high, low


def ring_tile(place, peers):
    if peers % 2:
        return place
    return jnp.where(place < peers // 2, 2 * place, 2 * (peers - 1 - place) + 1)


def ring_place(tile, peers):
    if peers % 2:
        return tile
    return jnp.where(tile % 2 == 0, tile // 2, peers - 1 - tile // 2)


def remote(src, dst, send_sem, recv_sem, target):
    return pltpu.make_async_remote_copy(
        src_ref=src,
        dst_ref=dst,
        send_sem=send_sem,
        recv_sem=recv_sem,
        device_id=target,
        device_id_type=pl.DeviceIdType.MESH,
    )


def greet(peers, tile, lev):
    barrier = pltpu.get_barrier_semaphore()
    for offset in range(1, peers):
        pl.semaphore_signal(
            barrier,
            inc=1,
            device_id={"tile": lax.rem(tile + offset, peers)},
            device_id_type=pl.DeviceIdType.MESH,
        )
    pl.semaphore_signal(
        barrier, inc=1, device_id={"lev": 1 - lev}, device_id_type=pl.DeviceIdType.MESH
    )
    pl.semaphore_wait(barrier, peers)


def exchange_kernel(
    peers,
    group,
    members_ref,
    early_ref,
    late_ref,
    energy_ref,
    weight_ref,
    packed_ref,
    pert_ref,
    summary_ref,
    lookups_ref,
    perts_ref,
    members_buf,
    own_buf,
    sent_buf,
    other_buf,
    in_sem,
    out_sem,
    lev_send,
    lev_recv,
    look_send,
    look_recv,
    ring_send,
    ring_recv,
    local_sem,
):
    tile = lax.axis_index("tile")
    lev = lax.axis_index("lev")
    chunks, members, levels, width = members_buf.shape
    bins = own_buf.shape[1]
    share = perts_ref.shape[2]
    piece = share // 2
    place = ring_place(tile, peers)
    half = pl.multiple_of(lev * share, LANES)
    partner = {"lev": 1 - lev}

    def fetch(chunk):
        here = pl.ds(pl.multiple_of(chunk * width, LANES), width)
        return pltpu.make_async_copy(members_ref.at[:, :, here], members_buf.at[chunk], in_sem.at[chunk])

    for chunk in range(chunks):
        fetch(chunk).start()
    own_look = pltpu.make_async_copy(packed_ref, lookups_ref.at[tile], local_sem.at[0])
    own_look.start()
    own_pert = pltpu.make_async_copy(
        pert_ref.at[0, :, pl.ds(half, share)], perts_ref.at[tile], local_sem.at[1]
    )
    own_pert.start()
    greet(peers, tile, lev)

    look_copies = []
    for offset in range(1, peers):
        copy = remote(
            packed_ref,
            lookups_ref.at[tile],
            look_send.at[offset - 1],
            look_recv.at[offset - 1],
            {"tile": lax.rem(tile + offset, peers)},
        )
        copy.start()
        look_copies.append(copy)

    steps = peers // 2

    def ring_copy(way, step, part):
        towards = 1 if way == 0 else peers - 1
        holder = lax.rem(place + (peers - step if way == 0 else step), peers)
        block = ring_tile(holder, peers)
        if step == 0:
            src = pert_ref.at[0, :, pl.ds(pl.multiple_of(half + part * piece, LANES), piece)]
        else:
            src = perts_ref.at[block, :, pl.ds(part * piece, piece)]
        number = (way * steps + step) * 2 + part
        return remote(
            src,
            perts_ref.at[block, :, pl.ds(part * piece, piece)],
            ring_send.at[number],
            ring_recv.at[number],
            {"tile": ring_tile(lax.rem(place + towards, peers), peers)},
        )

    def parts_of(way, step):
        if peers % 2 == 0 and step == steps - 1:
            return (way,)
        return (0, 1)

    def ring_step(step):
        for part in (0, 1):
            for way in (0, 1):
                if step > 0 and part in parts_of(way, step - 1):
                    ring_copy(way, step - 1, part).wait_recv()
                if step < steps and part in parts_of(way, step):
                    ring_copy(way, step, part).start()

    if steps > 0:
        ring_step(0)

    def lev_copy(chunk):
        return remote(
            sent_buf.at[chunk], other_buf.at[chunk], lev_send.at[chunk], lev_recv.at[chunk], partner
        )

    rows = bins * group
    weight = jnp.concatenate(split_high_low(weight_ref[...]), axis=0)

    def compute(chunk, carry):
        fetch(chunk).wait()
        here = pl.ds(pl.multiple_of(chunk * width, LANES), width)
        scaled = energy_ref[:, here].astype(jnp.float32) * (
            early_ref[:, here].astype(jnp.float32) + late_ref[:, here].astype(jnp.float32)
        )
        for part in range(members // group):
            those = slice(part * group, (part + 1) * group)
            block = members_buf[chunk, those].astype(jnp.float32) * scaled[None]
            high, low = split_high_low(block.reshape(group * levels, width))
            both = jnp.dot(weight, high, preferred_element_type=jnp.float32)
            summed = both[:rows] + both[rows:]
            summed = summed + jnp.dot(weight[:rows], low, preferred_element_type=jnp.float32)
            shaped = summed.reshape(bins, group, width)
            own_buf[chunk, :, those, :] = shaped
            sent_buf[chunk, :, those, :] = shaped.astype(jnp.bfloat16)
        lev_copy(chunk).start()
        return carry

    lax.fori_loop(0, chunks, compute, 0)
    if steps > 1:
        ring_step(1)

    def finish(chunk):
        here = pl.ds(pl.multiple_of(chunk * width, LANES), width)
        return pltpu.make_async_copy(own_buf.at[chunk], summary_ref.at[:, :, here], out_sem.at[chunk])

    def add_other(chunk, carry):
        lev_copy(chunk).wait_recv()
        own_buf[chunk] = own_buf[chunk] + other_buf[chunk].astype(jnp.float32)
        finish(chunk).start()
        return carry

    lax.fori_loop(0, chunks, add_other, 0)
    for step in range(2, steps + 1):
        ring_step(step)
    if steps == 1:
        ring_step(1)
    for way in (0, 1):
        for step in range(steps):
            for part in parts_of(way, step):
                ring_copy(way, step, part).wait_send()
    for copy in look_copies:
        copy.wait()
    own_look.wait()
    own_pert.wait()
    for chunk in range(chunks):
        lev_copy(chunk).wait_send()
        finish(chunk).wait()


def exchange(members_x, error_early, error_late, energy, local_vert, packed, obs_pert, peers, share):
    members, levels, columns = members_x.shape
    bins = local_vert.shape[0]
    group = 16
    width = min(512, columns)
    chunks = columns // width
    ring = max(4 * (peers // 2), 1)
    eye = jnp.eye(group, dtype=jnp.float32)
    weight = (local_vert[:, None, None, :] * eye[None, :, :, None]).reshape(bins * group, group * levels)
    anywhere = pl.BlockSpec(memory_space=pl.ANY)
    near = pl.BlockSpec(memory_space=pltpu.VMEM)
    dma = pltpu.SemaphoreType.DMA
    return pl.pallas_call(
        functools.partial(exchange_kernel, peers, group),
        in_specs=[anywhere, near, near, near, near, near, anywhere],
        out_specs=[anywhere, anywhere, anywhere],
        out_shape=[
            jax.ShapeDtypeStruct((bins, members, columns), jnp.float32),
            jax.ShapeDtypeStruct((peers,) + packed.shape, jnp.int32),
            jax.ShapeDtypeStruct((peers, members, share), jnp.bfloat16),
        ],
        scratch_shapes=[
            pltpu.VMEM((chunks, members, levels, width), jnp.bfloat16),
            pltpu.VMEM((chunks, bins, members, width), jnp.float32),
            pltpu.VMEM((chunks, bins, members, width), jnp.bfloat16),
            pltpu.VMEM((chunks, bins, members, width), jnp.bfloat16),
            dma((chunks,)),
            dma((chunks,)),
            dma((chunks,)),
            dma((chunks,)),
            dma((max(peers - 1, 1),)),
            dma((max(peers - 1, 1),)),
            dma((ring,)),
            dma((ring,)),
            dma((2,)),
        ],
        compiler_params=pltpu.CompilerParams(
            vmem_limit_bytes=VMEM_LIMIT, collective_id=0, has_side_effects=True
        ),
        name="summary_exchange",
    )(members_x, error_early, error_late, energy, weight, packed, obs_pert)


def dots_kernel(bins, first_ref, last_ref, summary_ref, lookup_ref, pert_ref, dots_ref, table_ref, rows_ref):
    step = pl.program_id(0)
    members, columns = summary_ref.shape[1], summary_ref.shape[2]

    @pl.when(step < bins)
    def _():
        for start in range(0, columns, LANES):
            here = slice(start, start + LANES)
            summed = summary_ref[0, :, here]
            padded = jnp.concatenate(
                [summed, jnp.zeros((LANES - members, LANES), jnp.float32)], axis=0
            )
            place = pl.multiple_of(step * columns + start, LANES)
            table_ref[pl.ds(place, LANES), :] = padded.T

    @pl.when(step >= bins)
    def _():
        owner = step - bins
        dots_ref[...] = jnp.zeros_like(dots_ref)
        row_id = lax.broadcasted_iota(jnp.int32, (LANES, LANES), 0)
        col_id = lax.broadcasted_iota(jnp.int32, (LANES, LANES), 1)

        def one_chunk(chunk, carry):
            base = pl.multiple_of(chunk * CHUNK, CHUNK)
            for place in range(CHUNK):
                index = lookup_ref[0, 0, base + place]
                rows_ref[pl.ds(place, 1), :] = table_ref[pl.ds(index, 1), :]
            for sub in range(0, CHUNK, LANES):
                values = rows_ref[sub:sub + LANES, :members]
                high, low = split_high_low(values)
                here = pl.ds(pl.multiple_of(base + sub, LANES), LANES)
                pert = pert_ref[0, :, here]
                product = jnp.dot(high, pert, preferred_element_type=jnp.float32) + jnp.dot(
                    low, pert, preferred_element_type=jnp.float32
                )
                picked = jnp.where(row_id == col_id, product, 0.0)
                dots_ref[0, :, here] = jnp.sum(picked, axis=0, keepdims=True)
            return carry

        lax.fori_loop(first_ref[owner], last_ref[owner], one_chunk, 0)


def tile_dots(summary, lookups, perts, first, last):
    bins, members, columns = summary.shape
    peers, _, share = perts.shape
    return pl.pallas_call(
        functools.partial(dots_kernel, bins),
        grid_spec=pltpu.PrefetchScalarGridSpec(
            num_scalar_prefetch=2,
            grid=(bins + peers,),
            in_specs=[
                pl.BlockSpec((1, members, columns), lambda i, *_: (jnp.minimum(i, bins - 1), 0, 0)),
                pl.BlockSpec(
                    (1, 1, lookups.shape[2]), lambda i, *_: (jnp.maximum(i - bins, 0), 0, 0), memory_space=pltpu.SMEM
                ),
                pl.BlockSpec((1, members, share), lambda i, *_: (jnp.maximum(i - bins, 0), 0, 0)),
            ],
            out_specs=pl.BlockSpec((1, 1, share), lambda i, *_: (jnp.maximum(i - bins, 0), 0, 0)),
            scratch_shapes=[
                pltpu.VMEM((bins * columns, LANES), jnp.float32),
                pltpu.VMEM((CHUNK, LANES), jnp.float32),
            ],
        ),
        out_shape=jax.ShapeDtypeStruct((peers, 1, share), jnp.float32),
        compiler_params=pltpu.CompilerParams(vmem_limit_bytes=VMEM_LIMIT),
        name="tile_dots",
    )(first, last, summary, lookups, perts)


def combine_kernel(
    peers, dots_ref, weight_ref, scale_ref, out_ref, landed, send_sem, recv_sem, lev_send, lev_recv
):
    tile = lax.axis_index("tile")
    lev = lax.axis_index("lev")
    greet(peers, tile, lev)
    copies = []
    for offset in range(1, peers):
        target = lax.rem(tile + offset, peers)
        copy = remote(
            dots_ref.at[target],
            landed.at[tile],
            send_sem.at[offset - 1],
            recv_sem.at[offset - 1],
            {"tile": target},
        )
        copy.start()
        copies.append(copy)
    landed[tile] = dots_ref[tile]
    for copy in copies:
        copy.wait()
    total = jnp.zeros(scale_ref.shape, jnp.float32)
    for peer in range(peers):
        total = total + weight_ref[peer] * landed[peer]
    out_ref[lev] = scale_ref[...] * total
    swap = remote(out_ref.at[lev], out_ref.at[lev], lev_send, lev_recv, {"lev": 1 - lev})
    swap.start()
    swap.wait()


def combine(dots, weight, scale):
    peers, rows, lanes = dots.shape
    near = pl.BlockSpec(memory_space=pltpu.VMEM)
    dma = pltpu.SemaphoreType.DMA
    return pl.pallas_call(
        functools.partial(combine_kernel, peers),
        in_specs=[near, near, near],
        out_specs=near,
        out_shape=jax.ShapeDtypeStruct((2, rows, lanes), jnp.float32),
        scratch_shapes=[
            pltpu.VMEM((peers, rows, lanes), jnp.float32),
            dma((max(peers - 1, 1),)),
            dma((max(peers - 1, 1),)),
            dma,
            dma,
        ],
        compiler_params=pltpu.CompilerParams(
            vmem_limit_bytes=VMEM_LIMIT, collective_id=1, has_side_effects=True
        ),
        name="combine_dots",
    )(dots, weight, scale)


def on_device(
    members_x,
    error_early,
    error_late,
    energy,
    vert_weight,
    tile_lists,
    obs_block,
    obs_bin,
    obs_column,
    obs_pert,
    innovation,
    inv_variance,
    horiz_weight,
):
    lev_count = lax.axis_size("lev")
    lev_place = lax.axis_index("lev")
    peers = lax.axis_size("tile")
    tile_place = lax.axis_index("tile")
    members = members_x.shape[0]
    levels_here = members_x.shape[1]
    columns = members_x.shape[2]
    tile_table = tile_lists[0]
    blocks = tile_table.shape[0]
    later_slots = tile_table.shape[1]
    obs_count = obs_block.shape[1]
    share = obs_count // lev_count

    half = lev_place * share
    lookup = obs_bin[0] * columns + obs_column[0]
    lookup_half = lax.dynamic_slice_in_dim(lookup, half, share, 0)

    tile_ids = jnp.arange(peers, dtype=jnp.int32)
    block_ids = jnp.arange(blocks, dtype=jnp.int32)
    starts = jnp.sum((obs_block[0][None, :] < block_ids[:, None]).astype(jnp.int32), axis=1)
    ends = jnp.sum((obs_block[0][None, :] <= block_ids[:, None]).astype(jnp.int32), axis=1)
    listed = jnp.any(tile_table[:, :, None] == tile_ids[None, None, :], axis=1)
    range_first = jnp.sum(jnp.where(listed, starts[:, None], 0), axis=0)
    range_last = jnp.sum(jnp.where(listed, ends[:, None], 0), axis=0)
    range_first = jnp.where(tile_ids == tile_place, 0, range_first)
    range_last = jnp.where(tile_ids == tile_place, obs_count, range_last)
    range_first = jnp.clip(range_first - half, 0, share)
    range_last = jnp.clip(range_last - half, 0, share)
    spare = jnp.zeros(((-2 * peers) % LANES,), jnp.int32)
    packed = jnp.concatenate([lookup_half, range_first, range_last, spare])[None, :]

    local_vert = lax.dynamic_slice_in_dim(vert_weight, lev_place * levels_here, levels_here, 1)
    summary, everyone, perts = exchange(
        members_x, error_early, error_late, energy, local_vert, packed, obs_pert, peers, share
    )
    first = lax.dynamic_slice_in_dim(everyone[:, 0, share:share + peers], tile_place, 1, 1)[:, 0]
    last = lax.dynamic_slice_in_dim(everyone[:, 0, share + peers:share + 2 * peers], tile_place, 1, 1)[:, 0]
    first_chunk = first // CHUNK
    last_chunk = jnp.where(last > first, (last + CHUNK - 1) // CHUNK, first_chunk)
    dots = tile_dots(summary, everyone, perts, first_chunk, last_chunk)

    block_half = lax.dynamic_slice_in_dim(obs_block[0], half, share, 0)
    weight_half = lax.dynamic_slice_in_dim(horiz_weight[0], half, share, 1)
    weight = jnp.where(tile_ids[:, None] == tile_place, weight_half[0][None, :], 0.0)
    for block in range(blocks):
        for entry in range(later_slots):
            chosen = (tile_ids[:, None] == tile_table[block, entry]) & (block_half == block)[None, :]
            weight = weight + jnp.where(chosen, weight_half[entry + 1][None, :], 0.0)
    scale = lax.dynamic_slice_in_dim(innovation[0] * inv_variance[0], half, share, 0) / (members - 1.0)
    rows = share // LANES
    impact = combine(
        dots.reshape(peers, rows, LANES),
        weight.reshape(peers, rows, LANES),
        scale.reshape(rows, LANES),
    )
    impact = impact.reshape(obs_count // lev_count, lev_count).T
    impact = lax.dynamic_slice_in_dim(impact, lev_place, 1, 0)
    return impact[:, :, None]


def solution(mesh):
    return jax.shard_map(
        on_device,
        mesh=mesh,
        in_specs=(
            P(None, "lev", ("group", "tile")),
            P("lev", ("group", "tile")),
            P("lev", ("group", "tile")),
            P("lev", ("group", "tile")),
            P(),
            P(("group", "tile"), None, None),
            P(("group", "tile"), None),
            P(("group", "tile"), None),
            P(("group", "tile"), None),
            P(("group", "tile"), None, None),
            P(("group", "tile"), None),
            P(("group", "tile"), None),
            P(("group", "tile"), None, None),
        ),
        out_specs=P(("group", "tile"), None, "lev"),
        check_vma=False,
    )
```

```python
import functools

import jax
import jax.numpy as jnp
from jax import lax
from jax.experimental import pallas as pl
from jax.experimental.pallas import tpu as pltpu
from jax.sharding import PartitionSpec as P

CHUNK = 256
LANES = 128
VMEM_LIMIT = 56 * 1024 * 1024


def split_high_low(values):
    high = values.astype(jnp.bfloat16)
    low = (values - high.astype(jnp.float32)).astype(jnp.bfloat16)
    return high, low


def ring_tile(place, peers):
    if peers % 2:
        return place
    return jnp.where(place < peers // 2, 2 * place, 2 * (peers - 1 - place) + 1)


def ring_place(tile, peers):
    if peers % 2:
        return tile
    return jnp.where(tile % 2 == 0, tile // 2, peers - 1 - tile // 2)


def remote(src, dst, send_sem, recv_sem, target):
    return pltpu.make_async_remote_copy(
        src_ref=src,
        dst_ref=dst,
        send_sem=send_sem,
        recv_sem=recv_sem,
        device_id=target,
        device_id_type=pl.DeviceIdType.MESH,
    )


def greet(peers, tile, lev):
    barrier = pltpu.get_barrier_semaphore()
    for offset in range(1, peers):
        pl.semaphore_signal(
            barrier,
            inc=1,
            device_id={"tile": lax.rem(tile + offset, peers)},
            device_id_type=pl.DeviceIdType.MESH,
        )
    pl.semaphore_signal(
        barrier, inc=1, device_id={"lev": 1 - lev}, device_id_type=pl.DeviceIdType.MESH
    )
    pl.semaphore_wait(barrier, peers)


def exchange_kernel(
    peers,
    group,
    members_ref,
    early_ref,
    late_ref,
    energy_ref,
    weight_ref,
    packed_ref,
    pert_ref,
    summary_ref,
    lookups_ref,
    perts_ref,
    members_buf,
    own_buf,
    sent_buf,
    other_buf,
    table_buf,
    in_sem,
    out_sem,
    lev_send,
    lev_recv,
    look_send,
    look_recv,
    ring_send,
    ring_recv,
    local_sem,
):
    tile = lax.axis_index("tile")
    lev = lax.axis_index("lev")
    chunks, members, levels, width = members_buf.shape
    bins = own_buf.shape[1]
    share = perts_ref.shape[2]
    piece = share // 2
    place = ring_place(tile, peers)
    half = pl.multiple_of(lev * share, LANES)
    partner = {"lev": 1 - lev}

    def fetch(chunk):
        here = pl.ds(pl.multiple_of(chunk * width, LANES), width)
        return pltpu.make_async_copy(members_ref.at[:, :, here], members_buf.at[chunk], in_sem.at[chunk])

    for chunk in range(chunks):
        fetch(chunk).start()
    own_look = pltpu.make_async_copy(packed_ref, lookups_ref.at[tile], local_sem.at[0])
    own_look.start()
    own_pert = pltpu.make_async_copy(
        pert_ref.at[0, :, pl.ds(half, share)], perts_ref.at[tile], local_sem.at[1]
    )
    own_pert.start()
    greet(peers, tile, lev)

    look_copies = []
    for offset in range(1, peers):
        copy = remote(
            packed_ref,
            lookups_ref.at[tile],
            look_send.at[offset - 1],
            look_recv.at[offset - 1],
            {"tile": lax.rem(tile + offset, peers)},
        )
        copy.start()
        look_copies.append(copy)

    steps = peers // 2

    def ring_copy(way, step, part):
        towards = 1 if way == 0 else peers - 1
        holder = lax.rem(place + (peers - step if way == 0 else step), peers)
        block = ring_tile(holder, peers)
        if step == 0:
            src = pert_ref.at[0, :, pl.ds(pl.multiple_of(half + part * piece, LANES), piece)]
        else:
            src = perts_ref.at[block, :, pl.ds(part * piece, piece)]
        number = (way * steps + step) * 2 + part
        return remote(
            src,
            perts_ref.at[block, :, pl.ds(part * piece, piece)],
            ring_send.at[number],
            ring_recv.at[number],
            {"tile": ring_tile(lax.rem(place + towards, peers), peers)},
        )

    def parts_of(way, step):
        if peers % 2 == 0 and step == steps - 1:
            return (way,)
        return (0, 1)

    def ring_step(step):
        for part in (0, 1):
            for way in (0, 1):
                if step > 0 and part in parts_of(way, step - 1):
                    ring_copy(way, step - 1, part).wait_recv()
                if step < steps and part in parts_of(way, step):
                    ring_copy(way, step, part).start()

    if steps > 0:
        ring_step(0)

    def lev_copy(chunk):
        return remote(
            sent_buf.at[chunk], other_buf.at[chunk], lev_send.at[chunk], lev_recv.at[chunk], partner
        )

    rows = bins * group
    weight = jnp.concatenate(split_high_low(weight_ref[...]), axis=0)

    def compute(chunk, carry):
        fetch(chunk).wait()
        here = pl.ds(pl.multiple_of(chunk * width, LANES), width)
        scaled = energy_ref[:, here].astype(jnp.float32) * (
            early_ref[:, here].astype(jnp.float32) + late_ref[:, here].astype(jnp.float32)
        )
        for part in range(members // group):
            those = slice(part * group, (part + 1) * group)
            block = members_buf[chunk, those].astype(jnp.float32) * scaled[None]
            high, low = split_high_low(block.reshape(group * levels, width))
            both = jnp.dot(weight, high, preferred_element_type=jnp.float32)
            summed = both[:rows] + both[rows:]
            summed = summed + jnp.dot(weight[:rows], low, preferred_element_type=jnp.float32)
            shaped = summed.reshape(bins, group, width)
            own_buf[chunk, :, those, :] = shaped
            sent_buf[chunk, :, those, :] = shaped.astype(jnp.bfloat16)
        lev_copy(chunk).start()
        return carry

    lax.fori_loop(0, chunks, compute, 0)
    if steps > 1:
        ring_step(1)

    def finish(chunk):
        here = pl.ds(pl.multiple_of(chunk * width, LANES), width)
        return pltpu.make_async_copy(
            table_buf.at[chunk], summary_ref.at[:, here, :], out_sem.at[chunk]
        )

    def add_other(chunk, carry):
        lev_copy(chunk).wait_recv()
        for bin_id in range(bins):
            for start in range(0, width, LANES):
                here = slice(start, start + LANES)
                summed = own_buf[chunk, bin_id, :, here] + other_buf[chunk, bin_id, :, here].astype(
                    jnp.float32
                )
                padded = jnp.concatenate(
                    [summed, jnp.zeros((LANES - members, LANES), jnp.float32)], axis=0
                )
                table_buf[chunk, bin_id, here, :] = padded.T
        finish(chunk).start()
        return carry

    lax.fori_loop(0, chunks // 2, add_other, 0)
    if steps > 2:
        ring_step(2)
    lax.fori_loop(chunks // 2, chunks, add_other, 0)
    for step in range(3, steps + 1):
        ring_step(step)
    if 1 <= steps <= 2:
        ring_step(steps)
    for way in (0, 1):
        for step in range(steps):
            for part in parts_of(way, step):
                ring_copy(way, step, part).wait_send()
    for copy in look_copies:
        copy.wait()
    own_look.wait()
    own_pert.wait()
    for chunk in range(chunks):
        lev_copy(chunk).wait_send()
        finish(chunk).wait()


def exchange(members_x, error_early, error_late, energy, local_vert, packed, obs_pert, peers, share):
    members, levels, columns = members_x.shape
    bins = local_vert.shape[0]
    group = 16
    width = min(512, columns)
    chunks = columns // width
    ring = max(4 * (peers // 2), 1)
    eye = jnp.eye(group, dtype=jnp.float32)
    weight = (local_vert[:, None, None, :] * eye[None, :, :, None]).reshape(bins * group, group * levels)
    anywhere = pl.BlockSpec(memory_space=pl.ANY)
    near = pl.BlockSpec(memory_space=pltpu.VMEM)
    dma = pltpu.SemaphoreType.DMA
    return pl.pallas_call(
        functools.partial(exchange_kernel, peers, group),
        in_specs=[anywhere, near, near, near, near, near, anywhere],
        out_specs=[anywhere, anywhere, anywhere],
        out_shape=[
            jax.ShapeDtypeStruct((bins, columns, LANES), jnp.float32),
            jax.ShapeDtypeStruct((peers,) + packed.shape, jnp.int32),
            jax.ShapeDtypeStruct((peers, members, share), jnp.bfloat16),
        ],
        scratch_shapes=[
            pltpu.VMEM((chunks, members, levels, width), jnp.bfloat16),
            pltpu.VMEM((chunks, bins, members, width), jnp.float32),
            pltpu.VMEM((chunks, bins, members, width), jnp.bfloat16),
            pltpu.VMEM((chunks, bins, members, width), jnp.bfloat16),
            pltpu.VMEM((chunks, bins, width, LANES), jnp.float32),
            dma((chunks,)),
            dma((chunks,)),
            dma((chunks,)),
            dma((chunks,)),
            dma((max(peers - 1, 1),)),
            dma((max(peers - 1, 1),)),
            dma((ring,)),
            dma((ring,)),
            dma((2,)),
        ],
        compiler_params=pltpu.CompilerParams(
            vmem_limit_bytes=VMEM_LIMIT, collective_id=0, has_side_effects=True
        ),
        name="summary_exchange",
    )(members_x, error_early, error_late, energy, weight, packed, obs_pert)


def dots_kernel(members, summary_ref, lookup_ref, pert_ref, dots_ref, table_ref, rows_ref, table_sem):
    owner = pl.program_id(0)
    peers = pl.num_programs(0)
    tile = lax.axis_index("tile")
    share = pert_ref.shape[2]

    @pl.when(owner == 0)
    def _():
        copy = pltpu.make_async_copy(summary_ref, table_ref, table_sem)
        copy.start()
        copy.wait()

    dots_ref[...] = jnp.zeros_like(dots_ref)
    row_id = lax.broadcasted_iota(jnp.int32, (LANES, LANES), 0)
    col_id = lax.broadcasted_iota(jnp.int32, (LANES, LANES), 1)
    first = lookup_ref[0, 0, share + tile]
    last = lookup_ref[0, 0, share + peers + tile]
    first_chunk = lax.div(first, CHUNK)
    last_chunk = jnp.where(last > first, lax.div(last + CHUNK - 1, CHUNK), first_chunk)

    def gather(chunk):
        base = pl.multiple_of(chunk * CHUNK, CHUNK)
        slot = lax.rem(chunk, 2)
        for place in range(0, CHUNK, 8):
            rows = [
                table_ref[pl.ds(lookup_ref[0, 0, base + place + k], 1), :] for k in range(8)
            ]
            rows_ref[slot, place:place + 8, :] = jnp.concatenate(rows, axis=0)

    def products(chunk):
        base = pl.multiple_of(chunk * CHUNK, CHUNK)
        slot = lax.rem(chunk, 2)
        for sub in range(0, CHUNK, LANES):
            values = rows_ref[slot, sub:sub + LANES, :members]
            high, low = split_high_low(values)
            here = pl.ds(pl.multiple_of(base + sub, LANES), LANES)
            pert = pert_ref[0, :, here]
            product = jnp.dot(high, pert, preferred_element_type=jnp.float32) + jnp.dot(
                low, pert, preferred_element_type=jnp.float32
            )
            picked = jnp.where(row_id == col_id, product, 0.0)
            dots_ref[0, :, here] = jnp.sum(picked, axis=0, keepdims=True)

    def one_chunk(chunk, carry):
        products(chunk - 1)
        gather(chunk)
        return carry

    @pl.when(last_chunk > first_chunk)
    def _():
        gather(first_chunk)
        lax.fori_loop(first_chunk + 1, last_chunk, one_chunk, 0)
        products(last_chunk - 1)


def tile_dots(summary, lookups, perts):
    peers, members, share = perts.shape
    return pl.pallas_call(
        functools.partial(dots_kernel, members),
        grid=(peers,),
        in_specs=[
            pl.BlockSpec(memory_space=pl.ANY),
            pl.BlockSpec((1, 1, lookups.shape[2]), lambda i: (i, 0, 0), memory_space=pltpu.SMEM),
            pl.BlockSpec((1, members, share), lambda i: (i, 0, 0)),
        ],
        out_specs=pl.BlockSpec((1, 1, share), lambda i: (i, 0, 0)),
        out_shape=jax.ShapeDtypeStruct((peers, 1, share), jnp.float32),
        scratch_shapes=[
            pltpu.VMEM(summary.shape, jnp.float32),
            pltpu.VMEM((2, CHUNK, LANES), jnp.float32),
            pltpu.SemaphoreType.DMA,
        ],
        compiler_params=pltpu.CompilerParams(vmem_limit_bytes=VMEM_LIMIT),
        name="tile_dots",
    )(summary, lookups, perts)


def combine_kernel(
    peers,
    members,
    dots_ref,
    lists_ref,
    block_ref,
    innovation_ref,
    variance_ref,
    horiz_ref,
    out_ref,
    landed,
    halves,
    send_sem,
    recv_sem,
    lev_send,
    lev_recv,
):
    tile = lax.axis_index("tile")
    lev = lax.axis_index("lev")
    share = dots_ref.shape[2]
    blocks, later_slots = lists_ref.shape[1], lists_ref.shape[2]
    greet(peers, tile, lev)
    copies = []
    for offset in range(1, peers):
        target = lax.rem(tile + offset, peers)
        copy = remote(
            dots_ref.at[target],
            landed.at[tile],
            send_sem.at[offset - 1],
            recv_sem.at[offset - 1],
            {"tile": target},
        )
        copy.start()
        copies.append(copy)
    here = pl.ds(pl.multiple_of(lev * share, LANES), share)
    block = block_ref[:, here]
    listed = []
    for entry in range(later_slots):
        peer = jnp.zeros(block.shape, jnp.int32)
        for number in range(blocks):
            peer = jnp.where(block == number, lists_ref[0, number, entry], peer)
        listed.append(peer)
    weights = [horiz_ref[0, entry:entry + 1, here] for entry in range(later_slots + 1)]
    scale = innovation_ref[:, here] * variance_ref[:, here] / (members - 1.0)
    total = weights[0] * dots_ref[tile]
    for offset in range(1, peers):
        copies[offset - 1].wait_recv()
        sender = lax.rem(tile + peers - offset, peers)
        weight = jnp.zeros(total.shape, jnp.float32)
        for entry in range(later_slots):
            weight = weight + jnp.where(listed[entry] == sender, weights[entry + 1], 0.0)
        total = total + weight * landed[sender]
    impact = scale * total
    rows = share // LANES
    for row in range(rows):
        halves[lev, row % 2, row // 2:row // 2 + 1, :] = impact[:, row * LANES:(row + 1) * LANES]
    swap = remote(halves.at[lev], halves.at[lev], lev_send, lev_recv, {"lev": 1 - lev})
    swap.start()
    from_id = lax.broadcasted_iota(jnp.int32, (LANES, LANES), 0)
    to_id = lax.broadcasted_iota(jnp.int32, (LANES, LANES), 1)
    wanted = 2 * to_id + lev
    even = jnp.where(from_id == wanted, 1.0, 0.0)
    odd = jnp.where(from_id == wanted - LANES, 1.0, 0.0)
    swap.wait()
    for place in range(2):
        out_ref[place] = jnp.dot(
            halves[place, 0], even, precision=lax.Precision.HIGHEST, preferred_element_type=jnp.float32
        ) + jnp.dot(
            halves[place, 1], odd, precision=lax.Precision.HIGHEST, preferred_element_type=jnp.float32
        )
    for copy in copies:
        copy.wait_send()


def combine(dots, tile_lists, obs_block, innovation, inv_variance, horiz_weight, members):
    peers, _, share = dots.shape
    rows = share // LANES
    near = pl.BlockSpec(memory_space=pltpu.VMEM)
    dma = pltpu.SemaphoreType.DMA
    return pl.pallas_call(
        functools.partial(combine_kernel, peers, members),
        in_specs=[near, pl.BlockSpec(memory_space=pltpu.SMEM), near, near, near, near],
        out_specs=near,
        out_shape=jax.ShapeDtypeStruct((2, rows // 2, LANES), jnp.float32),
        scratch_shapes=[
            pltpu.VMEM((peers, 1, share), jnp.float32),
            pltpu.VMEM((2, 2, rows // 2, LANES), jnp.float32),
            dma((max(peers - 1, 1),)),
            dma((max(peers - 1, 1),)),
            dma,
            dma,
        ],
        compiler_params=pltpu.CompilerParams(
            vmem_limit_bytes=VMEM_LIMIT, collective_id=1, has_side_effects=True
        ),
        name="combine_dots",
    )(dots, tile_lists, obs_block, innovation, inv_variance, horiz_weight)


def on_device(
    members_x,
    error_early,
    error_late,
    energy,
    vert_weight,
    tile_lists,
    obs_block,
    obs_bin,
    obs_column,
    obs_pert,
    innovation,
    inv_variance,
    horiz_weight,
):
    lev_count = lax.axis_size("lev")
    lev_place = lax.axis_index("lev")
    peers = lax.axis_size("tile")
    tile_place = lax.axis_index("tile")
    members = members_x.shape[0]
    levels_here = members_x.shape[1]
    columns = members_x.shape[2]
    tile_table = tile_lists[0]
    blocks = tile_table.shape[0]
    later_slots = tile_table.shape[1]
    obs_count = obs_block.shape[1]
    share = obs_count // lev_count

    half = lev_place * share
    lookup = obs_bin[0] * columns + obs_column[0]
    lookup_half = lax.dynamic_slice_in_dim(lookup, half, share, 0)

    tile_ids = jnp.arange(peers, dtype=jnp.int32)
    block_ids = jnp.arange(blocks, dtype=jnp.int32)
    starts = jnp.sum((obs_block[0][None, :] < block_ids[:, None]).astype(jnp.int32), axis=1)
    ends = jnp.sum((obs_block[0][None, :] <= block_ids[:, None]).astype(jnp.int32), axis=1)
    listed = jnp.any(tile_table[:, :, None] == tile_ids[None, None, :], axis=1)
    range_first = jnp.sum(jnp.where(listed, starts[:, None], 0), axis=0)
    range_last = jnp.sum(jnp.where(listed, ends[:, None], 0), axis=0)
    range_first = jnp.where(tile_ids == tile_place, 0, range_first)
    range_last = jnp.where(tile_ids == tile_place, obs_count, range_last)
    range_first = jnp.clip(range_first - half, 0, share)
    range_last = jnp.clip(range_last - half, 0, share)
    spare = jnp.zeros(((-2 * peers) % LANES,), jnp.int32)
    packed = jnp.concatenate([lookup_half, range_first, range_last, spare])[None, :]

    local_vert = lax.dynamic_slice_in_dim(vert_weight, lev_place * levels_here, levels_here, 1)
    summary, everyone, perts = exchange(
        members_x, error_early, error_late, energy, local_vert, packed, obs_pert, peers, share
    )
    table = summary.reshape(-1, LANES)
    dots = tile_dots(table, everyone, perts)
    impact = combine(dots, tile_lists, obs_block, innovation, inv_variance, horiz_weight, members)
    return impact.reshape(1, obs_count // lev_count, 1)


def solution(mesh):
    return jax.shard_map(
        on_device,
        mesh=mesh,
        in_specs=(
            P(None, "lev", ("group", "tile")),
            P("lev", ("group", "tile")),
            P("lev", ("group", "tile")),
            P("lev", ("group", "tile")),
            P(),
            P(("group", "tile"), None, None),
            P(("group", "tile"), None),
            P(("group", "tile"), None),
            P(("group", "tile"), None),
            P(("group", "tile"), None, None),
            P(("group", "tile"), None),
            P(("group", "tile"), None),
            P(("group", "tile"), None, None),
        ),
        out_specs=P(("group", "tile"), None, "lev"),
        check_vma=False,
    )
```

```python
import functools

import jax
import jax.numpy as jnp
from jax import lax
from jax.experimental import pallas as pl
from jax.experimental.pallas import tpu as pltpu
from jax.sharding import PartitionSpec as P

CHUNK = 256
LANES = 128
VMEM_LIMIT = 56 * 1024 * 1024


def split_high_low(values):
    high = values.astype(jnp.bfloat16)
    low = (values - high.astype(jnp.float32)).astype(jnp.bfloat16)
    return high, low


def ring_tile(place, peers):
    if peers % 2:
        return place
    return jnp.where(place < peers // 2, 2 * place, 2 * (peers - 1 - place) + 1)


def ring_place(tile, peers):
    if peers % 2:
        return tile
    return jnp.where(tile % 2 == 0, tile // 2, peers - 1 - tile // 2)


def remote(src, dst, send_sem, recv_sem, target):
    return pltpu.make_async_remote_copy(
        src_ref=src,
        dst_ref=dst,
        send_sem=send_sem,
        recv_sem=recv_sem,
        device_id=target,
        device_id_type=pl.DeviceIdType.MESH,
    )


def greet(peers, tile, lev):
    barrier = pltpu.get_barrier_semaphore()
    for offset in range(1, peers):
        pl.semaphore_signal(
            barrier,
            inc=1,
            device_id={"tile": lax.rem(tile + offset, peers)},
            device_id_type=pl.DeviceIdType.MESH,
        )
    pl.semaphore_signal(
        barrier, inc=1, device_id={"lev": 1 - lev}, device_id_type=pl.DeviceIdType.MESH
    )
    pl.semaphore_wait(barrier, peers)


def gather_rows(table_ref, lookup_ref, which, rows_ref, chunk):
    base = pl.multiple_of(chunk * CHUNK, CHUNK)
    slot = lax.rem(chunk, 2)
    for place in range(0, CHUNK, 8):
        rows = [
            table_ref[pl.ds(lookup_ref[which, 0, base + place + k], 1), :] for k in range(8)
        ]
        rows_ref[slot, place:place + 8, :] = jnp.concatenate(rows, axis=0)


def dot_rows(rows_ref, pert_ref, dots_ref, which, chunk):
    members = pert_ref.shape[1]
    base = pl.multiple_of(chunk * CHUNK, CHUNK)
    slot = lax.rem(chunk, 2)
    row_id = lax.broadcasted_iota(jnp.int32, (LANES, LANES), 0)
    col_id = lax.broadcasted_iota(jnp.int32, (LANES, LANES), 1)
    for sub in range(0, CHUNK, LANES):
        high, low = split_high_low(rows_ref[slot, sub:sub + LANES, :members])
        here = pl.ds(pl.multiple_of(base + sub, LANES), LANES)
        pert = pert_ref[which, :, here]
        product = jnp.dot(high, pert, preferred_element_type=jnp.float32) + jnp.dot(
            low, pert, preferred_element_type=jnp.float32
        )
        picked = jnp.where(row_id == col_id, product, 0.0)
        dots_ref[which, :, here] = jnp.sum(picked, axis=0, keepdims=True)


def dots_of_chunks(table_ref, lookup_ref, rows_ref, pert_ref, dots_ref, which, first, last):
    def one_chunk(chunk, carry):
        dot_rows(rows_ref, pert_ref, dots_ref, which, chunk - 1)
        gather_rows(table_ref, lookup_ref, which, rows_ref, chunk)
        return carry

    gather_rows(table_ref, lookup_ref, which, rows_ref, first)
    lax.fori_loop(first + 1, last, one_chunk, 0)
    dot_rows(rows_ref, pert_ref, dots_ref, which, last - 1)


def exchange_kernel(
    peers,
    group,
    members_ref,
    early_ref,
    late_ref,
    energy_ref,
    weight_ref,
    packed_ref,
    pert_ref,
    summary_ref,
    lookups_ref,
    perts_ref,
    early_ref_out,
    members_buf,
    own_buf,
    sent_buf,
    other_buf,
    table_buf,
    look_buf,
    pert_buf,
    rows_buf,
    in_sem,
    out_sem,
    lev_send,
    lev_recv,
    look_send,
    look_recv,
    ring_send,
    ring_recv,
    local_sem,
    early_sem,
):
    tile = lax.axis_index("tile")
    lev = lax.axis_index("lev")
    chunks, members, levels, width = members_buf.shape
    bins = own_buf.shape[1]
    share = perts_ref.shape[2]
    piece = share // 2
    place = ring_place(tile, peers)
    half = pl.multiple_of(lev * share, LANES)
    partner = {"lev": 1 - lev}

    def fetch(chunk):
        here = pl.ds(pl.multiple_of(chunk * width, LANES), width)
        return pltpu.make_async_copy(members_ref.at[:, :, here], members_buf.at[chunk], in_sem.at[chunk])

    for chunk in range(chunks):
        fetch(chunk).start()
    own_look = pltpu.make_async_copy(packed_ref, lookups_ref.at[tile], local_sem.at[0])
    own_look.start()
    own_pert = pltpu.make_async_copy(
        pert_ref.at[0, :, pl.ds(half, share)], perts_ref.at[tile], local_sem.at[1]
    )
    own_pert.start()
    early_copies = [
        pltpu.make_async_copy(packed_ref, look_buf.at[0], early_sem.at[0]),
        pltpu.make_async_copy(pert_ref.at[0, :, pl.ds(half, share)], pert_buf.at[0], early_sem.at[1]),
    ]
    for copy in early_copies:
        copy.start()
    greet(peers, tile, lev)

    look_copies = []
    for offset in range(1, peers):
        copy = remote(
            packed_ref,
            lookups_ref.at[tile],
            look_send.at[offset - 1],
            look_recv.at[offset - 1],
            {"tile": lax.rem(tile + offset, peers)},
        )
        copy.start()
        look_copies.append(copy)

    steps = peers // 2

    def ring_copy(way, step, part):
        towards = 1 if way == 0 else peers - 1
        holder = lax.rem(place + (peers - step if way == 0 else step), peers)
        block = ring_tile(holder, peers)
        if step == 0:
            src = pert_ref.at[0, :, pl.ds(pl.multiple_of(half + part * piece, LANES), piece)]
        else:
            src = perts_ref.at[block, :, pl.ds(part * piece, piece)]
        number = (way * steps + step) * 2 + part
        return remote(
            src,
            perts_ref.at[block, :, pl.ds(part * piece, piece)],
            ring_send.at[number],
            ring_recv.at[number],
            {"tile": ring_tile(lax.rem(place + towards, peers), peers)},
        )

    def parts_of(way, step):
        if peers % 2 == 0 and step == steps - 1:
            return (way,)
        return (0, 1)

    def ring_step(step):
        for part in (0, 1):
            for way in (0, 1):
                if step > 0 and part in parts_of(way, step - 1):
                    ring_copy(way, step - 1, part).wait_recv()
                if step < steps and part in parts_of(way, step):
                    ring_copy(way, step, part).start()

    if steps > 0:
        ring_step(0)

    def lev_copy(chunk):
        return remote(
            sent_buf.at[chunk], other_buf.at[chunk], lev_send.at[chunk], lev_recv.at[chunk], partner
        )

    rows = bins * group
    weight = jnp.concatenate(split_high_low(weight_ref[...]), axis=0)

    def compute(chunk, carry):
        fetch(chunk).wait()
        here = pl.ds(pl.multiple_of(chunk * width, LANES), width)
        scaled = energy_ref[:, here].astype(jnp.float32) * (
            early_ref[:, here].astype(jnp.float32) + late_ref[:, here].astype(jnp.float32)
        )
        for part in range(members // group):
            those = slice(part * group, (part + 1) * group)
            block = members_buf[chunk, those].astype(jnp.float32) * scaled[None]
            high, low = split_high_low(block.reshape(group * levels, width))
            both = jnp.dot(weight, high, preferred_element_type=jnp.float32)
            summed = both[:rows] + both[rows:]
            summed = summed + jnp.dot(weight[:rows], low, preferred_element_type=jnp.float32)
            shaped = summed.reshape(bins, group, width)
            own_buf[chunk, :, those, :] = shaped
            sent_buf[chunk, :, those, :] = shaped.astype(jnp.bfloat16)
        lev_copy(chunk).start()
        return carry

    lax.fori_loop(0, chunks, compute, 0)
    if steps > 1:
        ring_step(1)

    for copy in look_copies:
        copy.wait_recv()
    neighbours = (lax.rem(place + peers - 1, peers), lax.rem(place + 1, peers)) if steps > 1 else ()
    for number, neighbour in enumerate(neighbours, 1):
        block = ring_tile(neighbour, peers)
        early_copies += [
            pltpu.make_async_copy(lookups_ref.at[block], look_buf.at[number], early_sem.at[2 * number]),
            pltpu.make_async_copy(perts_ref.at[block], pert_buf.at[number], early_sem.at[2 * number + 1]),
        ]
    for copy in early_copies[2:]:
        copy.start()

    def add_other(chunk, carry):
        lev_copy(chunk).wait_recv()
        for bin_id in range(bins):
            for start in range(0, width, LANES):
                here = slice(start, start + LANES)
                summed = own_buf[chunk, bin_id, :, here] + other_buf[chunk, bin_id, :, here].astype(
                    jnp.float32
                )
                padded = jnp.concatenate(
                    [summed, jnp.zeros((LANES - members, LANES), jnp.float32)], axis=0
                )
                row = pl.multiple_of(bin_id * chunks * width + chunk * width + start, LANES)
                table_buf[pl.ds(row, LANES), :] = padded.T
        return carry

    lax.fori_loop(0, chunks // 2, add_other, 0)
    if steps > 2:
        ring_step(2)
    lax.fori_loop(chunks // 2, chunks, add_other, 0)
    table_out = pltpu.make_async_copy(table_buf, summary_ref, out_sem)
    table_out.start()

    def early_dots(number):
        for copy in early_copies[2 * number:2 * number + 2]:
            copy.wait()
        dots_of_chunks(
            table_buf, look_buf, rows_buf, pert_buf, early_ref_out, number, 0, share // CHUNK
        )

    early_dots(0)
    if steps > 3:
        ring_step(3)
    for number in range(1, len(neighbours) + 1):
        early_dots(number)
    for step in range(4 if steps > 3 else 3, steps + 1):
        ring_step(step)
    if 1 <= steps <= 2:
        ring_step(steps)
    for way in (0, 1):
        for step in range(steps):
            for part in parts_of(way, step):
                ring_copy(way, step, part).wait_send()
    for copy in look_copies:
        copy.wait_send()
    own_look.wait()
    own_pert.wait()
    for chunk in range(chunks):
        lev_copy(chunk).wait_send()
    table_out.wait()


def exchange(members_x, error_early, error_late, energy, local_vert, packed, obs_pert, peers, share):
    members, levels, columns = members_x.shape
    bins = local_vert.shape[0]
    group = 16
    width = min(512, columns)
    chunks = columns // width
    ring = max(4 * (peers // 2), 1)
    eye = jnp.eye(group, dtype=jnp.float32)
    weight = (local_vert[:, None, None, :] * eye[None, :, :, None]).reshape(bins * group, group * levels)
    anywhere = pl.BlockSpec(memory_space=pl.ANY)
    near = pl.BlockSpec(memory_space=pltpu.VMEM)
    dma = pltpu.SemaphoreType.DMA
    return pl.pallas_call(
        functools.partial(exchange_kernel, peers, group),
        in_specs=[anywhere, near, near, near, near, anywhere, anywhere],
        out_specs=[anywhere, anywhere, anywhere, near],
        out_shape=[
            jax.ShapeDtypeStruct((bins * columns, LANES), jnp.float32),
            jax.ShapeDtypeStruct((peers,) + packed.shape, jnp.int32),
            jax.ShapeDtypeStruct((peers, members, share), jnp.bfloat16),
            jax.ShapeDtypeStruct((3, 1, share), jnp.float32),
        ],
        scratch_shapes=[
            pltpu.VMEM((chunks, members, levels, width), jnp.bfloat16),
            pltpu.VMEM((chunks, bins, members, width), jnp.float32),
            pltpu.VMEM((chunks, bins, members, width), jnp.bfloat16),
            pltpu.VMEM((chunks, bins, members, width), jnp.bfloat16),
            pltpu.VMEM((bins * columns, LANES), jnp.float32),
            pltpu.SMEM((3,) + packed.shape, jnp.int32),
            pltpu.VMEM((3, members, share), jnp.bfloat16),
            pltpu.VMEM((2, CHUNK, LANES), jnp.float32),
            dma((chunks,)),
            dma,
            dma((chunks,)),
            dma((chunks,)),
            dma((max(peers - 1, 1),)),
            dma((max(peers - 1, 1),)),
            dma((ring,)),
            dma((ring,)),
            dma((2,)),
            dma((6,)),
        ],
        compiler_params=pltpu.CompilerParams(
            vmem_limit_bytes=VMEM_LIMIT, collective_id=0, has_side_effects=True
        ),
        name="summary_exchange",
    )(members_x, error_early, error_late, energy, weight, packed, obs_pert)


def dots_kernel(
    peers, summary_ref, lookup_ref, pert_ref, early_ref, dots_ref, table_ref, rows_ref, table_sem
):
    owner = pl.program_id(0)
    tile = lax.axis_index("tile")
    share = pert_ref.shape[2]

    @pl.when(owner == 0)
    def _():
        copy = pltpu.make_async_copy(summary_ref, table_ref, table_sem)
        copy.start()
        copy.wait()

    apart = lax.rem(ring_place(owner, peers) - ring_place(tile, peers) + peers, peers)
    ready = (apart == 0) | (((apart == 1) | (apart == peers - 1)) & (peers > 3))

    @pl.when(ready)
    def _():
        dots_ref[0] = early_ref[jnp.where(apart == 0, 0, jnp.where(apart == 1, 2, 1))]

    @pl.when(jnp.logical_not(ready))
    def _():
        dots_ref[...] = jnp.zeros_like(dots_ref)
        first = lookup_ref[0, 0, share + tile]
        last = lookup_ref[0, 0, share + peers + tile]

        @pl.when(last > first)
        def _():
            dots_of_chunks(
                table_ref,
                lookup_ref,
                rows_ref,
                pert_ref,
                dots_ref,
                0,
                lax.div(first, CHUNK),
                lax.div(last + CHUNK - 1, CHUNK),
            )


def tile_dots(summary, lookups, perts, early):
    peers, members, share = perts.shape
    return pl.pallas_call(
        functools.partial(dots_kernel, peers),
        grid=(peers,),
        in_specs=[
            pl.BlockSpec(memory_space=pl.ANY),
            pl.BlockSpec((1, 1, lookups.shape[2]), lambda i: (i, 0, 0), memory_space=pltpu.SMEM),
            pl.BlockSpec((1, members, share), lambda i: (i, 0, 0)),
            pl.BlockSpec(early.shape, lambda i: (0, 0, 0)),
        ],
        out_specs=pl.BlockSpec((1, 1, share), lambda i: (i, 0, 0)),
        out_shape=jax.ShapeDtypeStruct((peers, 1, share), jnp.float32),
        scratch_shapes=[
            pltpu.VMEM(summary.shape, jnp.float32),
            pltpu.VMEM((2, CHUNK, LANES), jnp.float32),
            pltpu.SemaphoreType.DMA,
        ],
        compiler_params=pltpu.CompilerParams(vmem_limit_bytes=VMEM_LIMIT),
        name="tile_dots",
    )(summary, lookups, perts, early)


def combine_kernel(
    peers,
    members,
    dots_ref,
    lists_ref,
    block_ref,
    innovation_ref,
    variance_ref,
    horiz_ref,
    out_ref,
    landed,
    halves,
    send_sem,
    recv_sem,
    lev_send,
    lev_recv,
):
    tile = lax.axis_index("tile")
    lev = lax.axis_index("lev")
    share = dots_ref.shape[2]
    blocks, later_slots = lists_ref.shape[1], lists_ref.shape[2]
    greet(peers, tile, lev)
    copies = []
    for offset in range(1, peers):
        target = lax.rem(tile + offset, peers)
        copy = remote(
            dots_ref.at[target],
            landed.at[tile],
            send_sem.at[offset - 1],
            recv_sem.at[offset - 1],
            {"tile": target},
        )
        copy.start()
        copies.append(copy)
    here = pl.ds(pl.multiple_of(lev * share, LANES), share)
    block = block_ref[:, here]
    listed = []
    for entry in range(later_slots):
        peer = jnp.zeros(block.shape, jnp.int32)
        for number in range(blocks):
            peer = jnp.where(block == number, lists_ref[0, number, entry], peer)
        listed.append(peer)
    weights = [horiz_ref[0, entry:entry + 1, here] for entry in range(later_slots + 1)]
    scale = innovation_ref[:, here] * variance_ref[:, here] / (members - 1.0)
    total = weights[0] * dots_ref[tile]
    for offset in range(1, peers):
        copies[offset - 1].wait_recv()
        sender = lax.rem(tile + peers - offset, peers)
        weight = jnp.zeros(total.shape, jnp.float32)
        for entry in range(later_slots):
            weight = weight + jnp.where(listed[entry] == sender, weights[entry + 1], 0.0)
        total = total + weight * landed[sender]
    impact = scale * total
    rows = share // LANES
    for row in range(rows):
        halves[lev, row % 2, row // 2:row // 2 + 1, :] = impact[:, row * LANES:(row + 1) * LANES]
    swap = remote(halves.at[lev], halves.at[lev], lev_send, lev_recv, {"lev": 1 - lev})
    swap.start()
    from_id = lax.broadcasted_iota(jnp.int32, (LANES, LANES), 0)
    to_id = lax.broadcasted_iota(jnp.int32, (LANES, LANES), 1)
    wanted = 2 * to_id + lev
    even = jnp.where(from_id == wanted, 1.0, 0.0)
    odd = jnp.where(from_id == wanted - LANES, 1.0, 0.0)
    swap.wait()
    for place in range(2):
        out_ref[place] = jnp.dot(
            halves[place, 0], even, precision=lax.Precision.HIGHEST, preferred_element_type=jnp.float32
        ) + jnp.dot(
            halves[place, 1], odd, precision=lax.Precision.HIGHEST, preferred_element_type=jnp.float32
        )
    for copy in copies:
        copy.wait_send()


def combine(dots, tile_lists, obs_block, innovation, inv_variance, horiz_weight, members):
    peers, _, share = dots.shape
    rows = share // LANES
    near = pl.BlockSpec(memory_space=pltpu.VMEM)
    dma = pltpu.SemaphoreType.DMA
    return pl.pallas_call(
        functools.partial(combine_kernel, peers, members),
        in_specs=[near, pl.BlockSpec(memory_space=pltpu.SMEM), near, near, near, near],
        out_specs=near,
        out_shape=jax.ShapeDtypeStruct((2, rows // 2, LANES), jnp.float32),
        scratch_shapes=[
            pltpu.VMEM((peers, 1, share), jnp.float32),
            pltpu.VMEM((2, 2, rows // 2, LANES), jnp.float32),
            dma((max(peers - 1, 1),)),
            dma((max(peers - 1, 1),)),
            dma,
            dma,
        ],
        compiler_params=pltpu.CompilerParams(
            vmem_limit_bytes=VMEM_LIMIT, collective_id=1, has_side_effects=True
        ),
        name="combine_dots",
    )(dots, tile_lists, obs_block, innovation, inv_variance, horiz_weight)


def on_device(
    members_x,
    error_early,
    error_late,
    energy,
    vert_weight,
    tile_lists,
    obs_block,
    obs_bin,
    obs_column,
    obs_pert,
    innovation,
    inv_variance,
    horiz_weight,
):
    lev_count = lax.axis_size("lev")
    lev_place = lax.axis_index("lev")
    peers = lax.axis_size("tile")
    tile_place = lax.axis_index("tile")
    members = members_x.shape[0]
    levels_here = members_x.shape[1]
    columns = members_x.shape[2]
    tile_table = tile_lists[0]
    blocks = tile_table.shape[0]
    later_slots = tile_table.shape[1]
    obs_count = obs_block.shape[1]
    share = obs_count // lev_count

    half = lev_place * share
    lookup = obs_bin[0] * columns + obs_column[0]
    lookup_half = lax.dynamic_slice_in_dim(lookup, half, share, 0)

    tile_ids = jnp.arange(peers, dtype=jnp.int32)
    block_ids = jnp.arange(blocks, dtype=jnp.int32)
    starts = jnp.sum((obs_block[0][None, :] < block_ids[:, None]).astype(jnp.int32), axis=1)
    ends = jnp.sum((obs_block[0][None, :] <= block_ids[:, None]).astype(jnp.int32), axis=1)
    listed = jnp.any(tile_table[:, :, None] == tile_ids[None, None, :], axis=1)
    range_first = jnp.sum(jnp.where(listed, starts[:, None], 0), axis=0)
    range_last = jnp.sum(jnp.where(listed, ends[:, None], 0), axis=0)
    range_first = jnp.where(tile_ids == tile_place, 0, range_first)
    range_last = jnp.where(tile_ids == tile_place, obs_count, range_last)
    range_first = jnp.clip(range_first - half, 0, share)
    range_last = jnp.clip(range_last - half, 0, share)
    spare = jnp.zeros(((-2 * peers) % LANES,), jnp.int32)
    packed = jnp.concatenate([lookup_half, range_first, range_last, spare])[None, :]

    local_vert = lax.dynamic_slice_in_dim(vert_weight, lev_place * levels_here, levels_here, 1)
    summary, everyone, perts, early = exchange(
        members_x, error_early, error_late, energy, local_vert, packed, obs_pert, peers, share
    )
    dots = tile_dots(summary, everyone, perts, early)
    impact = combine(dots, tile_lists, obs_block, innovation, inv_variance, horiz_weight, members)
    return impact.reshape(1, obs_count // lev_count, 1)


def solution(mesh):
    return jax.shard_map(
        on_device,
        mesh=mesh,
        in_specs=(
            P(None, "lev", ("group", "tile")),
            P("lev", ("group", "tile")),
            P("lev", ("group", "tile")),
            P("lev", ("group", "tile")),
            P(),
            P(("group", "tile"), None, None),
            P(("group", "tile"), None),
            P(("group", "tile"), None),
            P(("group", "tile"), None),
            P(("group", "tile"), None, None),
            P(("group", "tile"), None),
            P(("group", "tile"), None),
            P(("group", "tile"), None, None),
        ),
        out_specs=P(("group", "tile"), None, "lev"),
        check_vma=False,
    )
```

```python
import functools

import jax
import jax.numpy as jnp
from jax import lax
from jax.experimental import pallas as pl
from jax.experimental.pallas import tpu as pltpu
from jax.sharding import PartitionSpec as P

CHUNK = 256
LANES = 128
VMEM_LIMIT = 56 * 1024 * 1024


def split_high_low(values):
    high = values.astype(jnp.bfloat16)
    low = (values - high.astype(jnp.float32)).astype(jnp.bfloat16)
    return high, low


def ring_tile(place, peers):
    if peers % 2:
        return place
    return jnp.where(place < peers // 2, 2 * place, 2 * (peers - 1 - place) + 1)


def ring_place(tile, peers):
    if peers % 2:
        return tile
    return jnp.where(tile % 2 == 0, tile // 2, peers - 1 - tile // 2)


def remote(src, dst, send_sem, recv_sem, target):
    return pltpu.make_async_remote_copy(
        src_ref=src,
        dst_ref=dst,
        send_sem=send_sem,
        recv_sem=recv_sem,
        device_id=target,
        device_id_type=pl.DeviceIdType.MESH,
    )


def greet(peers, tile, lev):
    barrier = pltpu.get_barrier_semaphore()
    for offset in range(1, peers):
        pl.semaphore_signal(
            barrier,
            inc=1,
            device_id={"tile": lax.rem(tile + offset, peers)},
            device_id_type=pl.DeviceIdType.MESH,
        )
    pl.semaphore_signal(
        barrier, inc=1, device_id={"lev": 1 - lev}, device_id_type=pl.DeviceIdType.MESH
    )
    pl.semaphore_wait(barrier, peers)


def gather_rows(table_ref, lookup_ref, which, rows_ref, chunk):
    base = pl.multiple_of(chunk * CHUNK, CHUNK)
    slot = lax.rem(chunk, 2)
    for place in range(0, CHUNK, 8):
        rows = [
            table_ref[pl.ds(lookup_ref[which, 0, base + place + k], 1), :] for k in range(8)
        ]
        rows_ref[slot, place:place + 8, :] = jnp.concatenate(rows, axis=0)


def dot_rows(rows_ref, pert_ref, dots_ref, which, chunk):
    members = pert_ref.shape[1]
    base = pl.multiple_of(chunk * CHUNK, CHUNK)
    slot = lax.rem(chunk, 2)
    row_id = lax.broadcasted_iota(jnp.int32, (LANES, LANES), 0)
    col_id = lax.broadcasted_iota(jnp.int32, (LANES, LANES), 1)
    for sub in range(0, CHUNK, LANES):
        high, low = split_high_low(rows_ref[slot, sub:sub + LANES, :members])
        here = pl.ds(pl.multiple_of(base + sub, LANES), LANES)
        pert = pert_ref[which, :, here]
        product = jnp.dot(high, pert, preferred_element_type=jnp.float32) + jnp.dot(
            low, pert, preferred_element_type=jnp.float32
        )
        picked = jnp.where(row_id == col_id, product, 0.0)
        dots_ref[which, :, here] = jnp.sum(picked, axis=0, keepdims=True)


def dots_of_chunks(table_ref, lookup_ref, rows_ref, pert_ref, dots_ref, which, first, last):
    def one_chunk(chunk, carry):
        dot_rows(rows_ref, pert_ref, dots_ref, which, chunk - 1)
        gather_rows(table_ref, lookup_ref, which, rows_ref, chunk)
        return carry

    gather_rows(table_ref, lookup_ref, which, rows_ref, first)
    lax.fori_loop(first + 1, last, one_chunk, 0)
    dot_rows(rows_ref, pert_ref, dots_ref, which, last - 1)


def exchange_kernel(
    peers,
    group,
    members_ref,
    early_ref,
    late_ref,
    energy_ref,
    weight_ref,
    packed_ref,
    pert_ref,
    summary_ref,
    lookups_ref,
    perts_ref,
    early_ref_out,
    members_buf,
    own_buf,
    sent_buf,
    other_buf,
    table_buf,
    look_buf,
    pert_buf,
    rows_buf,
    in_sem,
    out_sem,
    lev_send,
    lev_recv,
    look_send,
    look_recv,
    ring_send,
    ring_recv,
    local_sem,
    early_sem,
):
    tile = lax.axis_index("tile")
    lev = lax.axis_index("lev")
    chunks, members, levels, width = members_buf.shape
    bins = own_buf.shape[1]
    share = perts_ref.shape[2]
    piece = share // 2
    place = ring_place(tile, peers)
    half = pl.multiple_of(lev * share, LANES)
    partner = {"lev": 1 - lev}

    def fetch(chunk):
        here = pl.ds(pl.multiple_of(chunk * width, LANES), width)
        return pltpu.make_async_copy(members_ref.at[:, :, here], members_buf.at[chunk], in_sem.at[chunk])

    for chunk in range(chunks):
        fetch(chunk).start()
    own_look = pltpu.make_async_copy(packed_ref, lookups_ref.at[tile], local_sem.at[0])
    own_look.start()
    own_pert = pltpu.make_async_copy(
        pert_ref.at[0, :, pl.ds(half, share)], perts_ref.at[tile], local_sem.at[1]
    )
    own_pert.start()
    early_copies = [
        pltpu.make_async_copy(packed_ref, look_buf.at[0], early_sem.at[0]),
        pltpu.make_async_copy(pert_ref.at[0, :, pl.ds(half, share)], pert_buf.at[0], early_sem.at[1]),
    ]
    for copy in early_copies:
        copy.start()
    greet(peers, tile, lev)

    look_copies = []
    for offset in range(1, peers):
        copy = remote(
            packed_ref,
            lookups_ref.at[tile],
            look_send.at[offset - 1],
            look_recv.at[offset - 1],
            {"tile": lax.rem(tile + offset, peers)},
        )
        copy.start()
        look_copies.append(copy)

    steps = peers // 2

    def ring_copy(way, step, part):
        towards = 1 if way == 0 else peers - 1
        holder = lax.rem(place + (peers - step if way == 0 else step), peers)
        block = ring_tile(holder, peers)
        if step == 0:
            src = pert_ref.at[0, :, pl.ds(pl.multiple_of(half + part * piece, LANES), piece)]
        else:
            src = perts_ref.at[block, :, pl.ds(part * piece, piece)]
        number = (way * steps + step) * 2 + part
        return remote(
            src,
            perts_ref.at[block, :, pl.ds(part * piece, piece)],
            ring_send.at[number],
            ring_recv.at[number],
            {"tile": ring_tile(lax.rem(place + towards, peers), peers)},
        )

    def parts_of(way, step):
        if peers % 2 == 0 and step == steps - 1:
            return (way,)
        return (0, 1)

    def ring_step(step):
        for part in (0, 1):
            for way in (0, 1):
                if step > 0 and part in parts_of(way, step - 1):
                    ring_copy(way, step - 1, part).wait_recv()
                if step < steps and part in parts_of(way, step):
                    ring_copy(way, step, part).start()

    if steps > 0:
        ring_step(0)

    def lev_copy(chunk):
        return remote(
            sent_buf.at[chunk], other_buf.at[chunk], lev_send.at[chunk], lev_recv.at[chunk], partner
        )

    rows = bins * group
    weight = jnp.concatenate(split_high_low(weight_ref[...]), axis=0)

    def compute(chunk, carry):
        fetch(chunk).wait()
        here = pl.ds(pl.multiple_of(chunk * width, LANES), width)
        scaled = energy_ref[:, here].astype(jnp.float32) * (
            early_ref[:, here].astype(jnp.float32) + late_ref[:, here].astype(jnp.float32)
        )
        for part in range(members // group):
            those = slice(part * group, (part + 1) * group)
            block = members_buf[chunk, those].astype(jnp.float32) * scaled[None]
            high, low = split_high_low(block.reshape(group * levels, width))
            both = jnp.dot(weight, high, preferred_element_type=jnp.float32)
            summed = both[:rows] + both[rows:]
            summed = summed + jnp.dot(weight[:rows], low, preferred_element_type=jnp.float32)
            shaped = summed.reshape(bins, group, width)
            own_buf[chunk, :, those, :] = shaped
            sent_buf[chunk, :, those, :] = shaped.astype(jnp.bfloat16)
        lev_copy(chunk).start()
        return carry

    lax.fori_loop(0, chunks, compute, 0)
    if steps > 1:
        ring_step(1)

    def add_other(chunk, carry):
        lev_copy(chunk).wait_recv()
        for bin_id in range(bins):
            for start in range(0, width, LANES):
                here = slice(start, start + LANES)
                summed = own_buf[chunk, bin_id, :, here] + other_buf[chunk, bin_id, :, here].astype(
                    jnp.float32
                )
                padded = jnp.concatenate(
                    [summed, jnp.zeros((LANES - members, LANES), jnp.float32)], axis=0
                )
                row = pl.multiple_of(bin_id * chunks * width + chunk * width + start, LANES)
                table_buf[pl.ds(row, LANES), :] = padded.T
        return carry

    lax.fori_loop(0, chunks // 2, add_other, 0)
    if steps > 2:
        ring_step(2)
    lax.fori_loop(chunks // 2, chunks, add_other, 0)
    table_out = pltpu.make_async_copy(table_buf, summary_ref, out_sem)
    table_out.start()

    if steps > 3:
        ring_step(3)
    for copy in early_copies:
        copy.wait()
    dots_of_chunks(
        table_buf, look_buf, rows_buf, pert_buf, early_ref_out, 0, 0, share // CHUNK
    )
    for step in range(4 if steps > 3 else 3, steps + 1):
        ring_step(step)
    if 1 <= steps <= 2:
        ring_step(steps)
    for way in (0, 1):
        for step in range(steps):
            for part in parts_of(way, step):
                ring_copy(way, step, part).wait_send()
    for copy in look_copies:
        copy.wait()
    own_look.wait()
    own_pert.wait()
    for chunk in range(chunks):
        lev_copy(chunk).wait_send()
    table_out.wait()


def exchange(members_x, error_early, error_late, energy, local_vert, packed, obs_pert, peers, share):
    members, levels, columns = members_x.shape
    bins = local_vert.shape[0]
    group = 16
    width = min(512, columns)
    chunks = columns // width
    ring = max(4 * (peers // 2), 1)
    eye = jnp.eye(group, dtype=jnp.float32)
    weight = (local_vert[:, None, None, :] * eye[None, :, :, None]).reshape(bins * group, group * levels)
    anywhere = pl.BlockSpec(memory_space=pl.ANY)
    near = pl.BlockSpec(memory_space=pltpu.VMEM)
    dma = pltpu.SemaphoreType.DMA
    return pl.pallas_call(
        functools.partial(exchange_kernel, peers, group),
        in_specs=[anywhere, near, near, near, near, anywhere, anywhere],
        out_specs=[anywhere, anywhere, anywhere, near],
        out_shape=[
            jax.ShapeDtypeStruct((bins * columns, LANES), jnp.float32),
            jax.ShapeDtypeStruct((peers,) + packed.shape, jnp.int32),
            jax.ShapeDtypeStruct((peers, members, share), jnp.bfloat16),
            jax.ShapeDtypeStruct((1, 1, share), jnp.float32),
        ],
        scratch_shapes=[
            pltpu.VMEM((chunks, members, levels, width), jnp.bfloat16),
            pltpu.VMEM((chunks, bins, members, width), jnp.float32),
            pltpu.VMEM((chunks, bins, members, width), jnp.bfloat16),
            pltpu.VMEM((chunks, bins, members, width), jnp.bfloat16),
            pltpu.VMEM((bins * columns, LANES), jnp.float32),
            pltpu.SMEM((1,) + packed.shape, jnp.int32),
            pltpu.VMEM((1, members, share), jnp.bfloat16),
            pltpu.VMEM((2, CHUNK, LANES), jnp.float32),
            dma((chunks,)),
            dma,
            dma((chunks,)),
            dma((chunks,)),
            dma((max(peers - 1, 1),)),
            dma((max(peers - 1, 1),)),
            dma((ring,)),
            dma((ring,)),
            dma((2,)),
            dma((2,)),
        ],
        compiler_params=pltpu.CompilerParams(
            vmem_limit_bytes=VMEM_LIMIT, collective_id=0, has_side_effects=True
        ),
        name="summary_exchange",
    )(members_x, error_early, error_late, energy, weight, packed, obs_pert)


def dots_kernel(
    peers, summary_ref, lookup_ref, pert_ref, early_ref, dots_ref, table_ref, rows_ref, table_sem
):
    owner = pl.program_id(0)
    tile = lax.axis_index("tile")
    share = pert_ref.shape[2]

    @pl.when(owner == 0)
    def _():
        copy = pltpu.make_async_copy(summary_ref, table_ref, table_sem)
        copy.start()
        copy.wait()

    ready = owner == tile

    @pl.when(ready)
    def _():
        dots_ref[0] = early_ref[0]

    @pl.when(jnp.logical_not(ready))
    def _():
        dots_ref[...] = jnp.zeros_like(dots_ref)
        first = lookup_ref[0, 0, share + tile]
        last = lookup_ref[0, 0, share + peers + tile]

        @pl.when(last > first)
        def _():
            dots_of_chunks(
                table_ref,
                lookup_ref,
                rows_ref,
                pert_ref,
                dots_ref,
                0,
                lax.div(first, CHUNK),
                lax.div(last + CHUNK - 1, CHUNK),
            )


def tile_dots(summary, lookups, perts, early):
    peers, members, share = perts.shape
    return pl.pallas_call(
        functools.partial(dots_kernel, peers),
        grid=(peers,),
        in_specs=[
            pl.BlockSpec(memory_space=pl.ANY),
            pl.BlockSpec((1, 1, lookups.shape[2]), lambda i: (i, 0, 0), memory_space=pltpu.SMEM),
            pl.BlockSpec((1, members, share), lambda i: (i, 0, 0)),
            pl.BlockSpec(early.shape, lambda i: (0, 0, 0)),
        ],
        out_specs=pl.BlockSpec((1, 1, share), lambda i: (i, 0, 0)),
        out_shape=jax.ShapeDtypeStruct((peers, 1, share), jnp.float32),
        scratch_shapes=[
            pltpu.VMEM(summary.shape, jnp.float32),
            pltpu.VMEM((2, CHUNK, LANES), jnp.float32),
            pltpu.SemaphoreType.DMA,
        ],
        compiler_params=pltpu.CompilerParams(vmem_limit_bytes=VMEM_LIMIT),
        name="tile_dots",
    )(summary, lookups, perts, early)


def combine_kernel(
    peers,
    members,
    dots_ref,
    lists_ref,
    block_ref,
    innovation_ref,
    variance_ref,
    horiz_ref,
    out_ref,
    landed,
    halves,
    send_sem,
    recv_sem,
    lev_send,
    lev_recv,
):
    tile = lax.axis_index("tile")
    lev = lax.axis_index("lev")
    share = dots_ref.shape[2]
    blocks, later_slots = lists_ref.shape[1], lists_ref.shape[2]
    greet(peers, tile, lev)
    copies = []
    for offset in range(1, peers):
        target = lax.rem(tile + offset, peers)
        copy = remote(
            dots_ref.at[target],
            landed.at[tile],
            send_sem.at[offset - 1],
            recv_sem.at[offset - 1],
            {"tile": target},
        )
        copy.start()
        copies.append(copy)
    here = pl.ds(pl.multiple_of(lev * share, LANES), share)
    block = block_ref[:, here]
    listed = []
    for entry in range(later_slots):
        peer = jnp.zeros(block.shape, jnp.int32)
        for number in range(blocks):
            peer = jnp.where(block == number, lists_ref[0, number, entry], peer)
        listed.append(peer)
    weights = [horiz_ref[0, entry:entry + 1, here] for entry in range(later_slots + 1)]
    scale = innovation_ref[:, here] * variance_ref[:, here] / (members - 1.0)
    total = weights[0] * dots_ref[tile]
    for offset in range(1, peers):
        copies[offset - 1].wait_recv()
        sender = lax.rem(tile + peers - offset, peers)
        weight = jnp.zeros(total.shape, jnp.float32)
        for entry in range(later_slots):
            weight = weight + jnp.where(listed[entry] == sender, weights[entry + 1], 0.0)
        total = total + weight * landed[sender]
    impact = scale * total
    rows = share // LANES
    for row in range(rows):
        halves[lev, row % 2, row // 2:row // 2 + 1, :] = impact[:, row * LANES:(row + 1) * LANES]
    swap = remote(halves.at[lev], halves.at[lev], lev_send, lev_recv, {"lev": 1 - lev})
    swap.start()
    from_id = lax.broadcasted_iota(jnp.int32, (LANES, LANES), 0)
    to_id = lax.broadcasted_iota(jnp.int32, (LANES, LANES), 1)
    wanted = 2 * to_id + lev
    even = jnp.where(from_id == wanted, 1.0, 0.0)
    odd = jnp.where(from_id == wanted - LANES, 1.0, 0.0)
    swap.wait()
    for place in range(2):
        out_ref[place] = jnp.dot(
            halves[place, 0], even, precision=lax.Precision.HIGHEST, preferred_element_type=jnp.float32
        ) + jnp.dot(
            halves[place, 1], odd, precision=lax.Precision.HIGHEST, preferred_element_type=jnp.float32
        )
    for copy in copies:
        copy.wait_send()


def combine(dots, tile_lists, obs_block, innovation, inv_variance, horiz_weight, members):
    peers, _, share = dots.shape
    rows = share // LANES
    near = pl.BlockSpec(memory_space=pltpu.VMEM)
    dma = pltpu.SemaphoreType.DMA
    return pl.pallas_call(
        functools.partial(combine_kernel, peers, members),
        in_specs=[near, pl.BlockSpec(memory_space=pltpu.SMEM), near, near, near, near],
        out_specs=near,
        out_shape=jax.ShapeDtypeStruct((2, rows // 2, LANES), jnp.float32),
        scratch_shapes=[
            pltpu.VMEM((peers, 1, share), jnp.float32),
            pltpu.VMEM((2, 2, rows // 2, LANES), jnp.float32),
            dma((max(peers - 1, 1),)),
            dma((max(peers - 1, 1),)),
            dma,
            dma,
        ],
        compiler_params=pltpu.CompilerParams(
            vmem_limit_bytes=VMEM_LIMIT, collective_id=1, has_side_effects=True
        ),
        name="combine_dots",
    )(dots, tile_lists, obs_block, innovation, inv_variance, horiz_weight)


def on_device(
    members_x,
    error_early,
    error_late,
    energy,
    vert_weight,
    tile_lists,
    obs_block,
    obs_bin,
    obs_column,
    obs_pert,
    innovation,
    inv_variance,
    horiz_weight,
):
    lev_count = lax.axis_size("lev")
    lev_place = lax.axis_index("lev")
    peers = lax.axis_size("tile")
    tile_place = lax.axis_index("tile")
    members = members_x.shape[0]
    levels_here = members_x.shape[1]
    columns = members_x.shape[2]
    tile_table = tile_lists[0]
    blocks = tile_table.shape[0]
    later_slots = tile_table.shape[1]
    obs_count = obs_block.shape[1]
    share = obs_count // lev_count

    half = lev_place * share
    lookup = obs_bin[0] * columns + obs_column[0]
    lookup_half = lax.dynamic_slice_in_dim(lookup, half, share, 0)

    tile_ids = jnp.arange(peers, dtype=jnp.int32)
    block_ids = jnp.arange(blocks, dtype=jnp.int32)
    starts = jnp.sum((obs_block[0][None, :] < block_ids[:, None]).astype(jnp.int32), axis=1)
    ends = jnp.sum((obs_block[0][None, :] <= block_ids[:, None]).astype(jnp.int32), axis=1)
    listed = jnp.any(tile_table[:, :, None] == tile_ids[None, None, :], axis=1)
    range_first = jnp.sum(jnp.where(listed, starts[:, None], 0), axis=0)
    range_last = jnp.sum(jnp.where(listed, ends[:, None], 0), axis=0)
    range_first = jnp.where(tile_ids == tile_place, 0, range_first)
    range_last = jnp.where(tile_ids == tile_place, obs_count, range_last)
    range_first = jnp.clip(range_first - half, 0, share)
    range_last = jnp.clip(range_last - half, 0, share)
    spare = jnp.zeros(((-2 * peers) % LANES,), jnp.int32)
    packed = jnp.concatenate([lookup_half, range_first, range_last, spare])[None, :]

    local_vert = lax.dynamic_slice_in_dim(vert_weight, lev_place * levels_here, levels_here, 1)
    summary, everyone, perts, early = exchange(
        members_x, error_early, error_late, energy, local_vert, packed, obs_pert, peers, share
    )
    dots = tile_dots(summary, everyone, perts, early)
    impact = combine(dots, tile_lists, obs_block, innovation, inv_variance, horiz_weight, members)
    return impact.reshape(1, obs_count // lev_count, 1)


def solution(mesh):
    return jax.shard_map(
        on_device,
        mesh=mesh,
        in_specs=(
            P(None, "lev", ("group", "tile")),
            P("lev", ("group", "tile")),
            P("lev", ("group", "tile")),
            P("lev", ("group", "tile")),
            P(),
            P(("group", "tile"), None, None),
            P(("group", "tile"), None),
            P(("group", "tile"), None),
            P(("group", "tile"), None),
            P(("group", "tile"), None, None),
            P(("group", "tile"), None),
            P(("group", "tile"), None),
            P(("group", "tile"), None, None),
        ),
        out_specs=P(("group", "tile"), None, "lev"),
        check_vma=False,
    )
```
